128 devices in a mesh: dp: 2 (over x_lo), tm: 64 (over z, y, x_hi, core).
Axes of the slice: x: 4 (x_hi: 2, x_lo: 2; x = x_hi * 2 + x_lo), y: 4, z: 4, core: 2. Of those that a mesh axis runs over, the one named last changes fastest.
Arguments:
- frames: bfloat16 [2, 64, 36, 64, 640], P('dp', 'tm'), may hold values from -8 to 8
- norm_gain: float32 [640], replicated, may hold values from 0.1 to 1.9
- norm_shift: float32 [640], replicated, may hold values from -1.5 to 1.5
- spatial_weight: bfloat16 [3, 3, 640, 640], P(None, None, 'dp'), may hold values from -0.078125 to 0.078125
- spatial_bias: float32 [640], replicated, may hold values from -1.5 to 1.5
- temporal_weight: bfloat16 [3, 640, 640], P(None, 'dp'), may hold values from -0.125 to 0.125
- temporal_bias: float32 [640], replicated, may hold values from -1.5 to 1.5
Outputs:
- block_out: bfloat16 [2, 64, 36, 64, 640], P('dp', 'tm')
The draws below stay inside these ranges and needn't reach their ends.
All inputs are finite; a program needn't handle non-finite values.
Results may differ from the reference program's by a relative error of at most 0.006.
Values may be sent and summed in bfloat16 or wider, within the bound.
A program may use at most 192 MiB of HBM per device.

```python
import jax
import jax.numpy as jnp
from jax import lax

D = 640
GROUPS = 32
HEIGHT = 36
WIDTH = 64
FRAMES = 64
CLIPS = 2


def draw_frames(key, part):
    key = jax.random.fold_in(key, 1)
    noise_key = jax.random.fold_in(key, 0)
    channel_key = jax.random.fold_in(key, 1)
    frame_key = jax.random.fold_in(key, 3)
    shift_key = jax.random.fold_in(key, 4)
    shape = (CLIPS, FRAMES, HEIGHT, WIDTH, D)
    per_group = D // GROUPS
    position = jnp.arange(FRAMES, dtype=jnp.float32) / max(FRAMES - 1, 1)
    rise = (0.5 + position).reshape(1, FRAMES, 1)
    frame_group = jnp.exp(jax.random.uniform(frame_key, (CLIPS, FRAMES, GROUPS), jnp.float32, -0.7, 0.7)) * rise
    frame_group = jnp.repeat(frame_group, per_group, axis=2).reshape(CLIPS, FRAMES, 1, 1, D)
    group_shift = jax.random.uniform(shift_key, (CLIPS, FRAMES, GROUPS), jnp.float32, -0.6, 0.6)
    group_shift = jnp.repeat(group_shift, per_group, axis=2).reshape(CLIPS, FRAMES, 1, 1, D)
    channel_scale = jnp.exp(jax.random.uniform(channel_key, (CLIPS, 1, 1, 1, D), jnp.float32, -0.5, 0.5))
    noise_base = jax.random.normal(noise_key, shape, jnp.float32)
    return jnp.clip((noise_base + group_shift) * frame_group * channel_scale, -8.0, 8.0).astype(jnp.bfloat16)


def steps_of(stream_key, dims, cuts, low, largest):
    def one(dim, blocks):
        draws = jax.random.uniform(jax.random.fold_in(jax.random.fold_in(stream_key, 6), dim), (blocks,), jnp.float32, low / len(cuts), largest / len(cuts))
        return jnp.repeat(jnp.exp(draws), dims[dim] // blocks).reshape((-1,) + (1,) * (len(dims) - dim - 1))

    loudness = one(*cuts[0])
    for cut in cuts[1:]:
        loudness = loudness * one(*cut)
    return loudness


def normal_values(rng, shape, spread, bound, pieces=(), kind=jnp.bfloat16):
    drawn = spread * jax.random.normal(rng, shape, jnp.float32)
    if pieces:
        drawn = drawn * steps_of(rng, shape, pieces, -0.22, 0.18)
    return jnp.clip(drawn, -bound, bound).astype(kind)


def setup_inputs(seed: int = 0) -> dict:
    streams_of = jax.random.split(jax.random.key(seed), 8)
    frames = draw_frames(jax.random.fold_in(streams_of[7], 71), 0)
    norm_gain = jnp.clip(1.0 + 0.18 * jax.random.normal(streams_of[1], (D,), jnp.float32), 0.1, 1.9)
    norm_shift = normal_values(streams_of[2], (D,), 0.3, 1.5, (), jnp.float32)
    spatial_weight = normal_values(streams_of[3], (3, 3, D, D), (9 * D) ** -0.5, 0.078125, ((2, 2),))
    spatial_bias = normal_values(streams_of[4], (D,), 0.3, 1.5, (), jnp.float32)
    temporal_weight = normal_values(streams_of[5], (3, D, D), (3 * D) ** -0.5, 0.125, ((1, 2),))
    temporal_bias = normal_values(streams_of[6], (D,), 0.3, 1.5, (), jnp.float32)
    return {"frames": frames, "norm_gain": norm_gain, "norm_shift": norm_shift, "spatial_weight": spatial_weight, "spatial_bias": spatial_bias, "temporal_weight": temporal_weight, "temporal_bias": temporal_bias}


def reference(frames, norm_gain, norm_shift, spatial_weight, spatial_bias, temporal_weight, temporal_bias):
    clip_count, frame_count, height, columns, channels = frames.shape
    per_group = channels // GROUPS
    signal = frames.astype(jnp.float32)
    grouped = signal.reshape(clip_count, frame_count, height, columns, GROUPS, per_group)
    members = frame_count * height * columns * per_group
    sum_values = lax.optimization_barrier(jnp.sum(grouped, axis=(1, 2, 3, 5)))
    sum_squares = lax.optimization_barrier(jnp.sum(grouped * grouped, axis=(1, 2, 3, 5)))
    average = sum_values / members
    variance = sum_squares / members - average * average
    inverse_std = lax.rsqrt(variance + 1e-05)
    normed = (grouped - average[:, None, None, None, :, None]) * inverse_std[:, None, None, None, :, None]
    normed = normed.reshape(clip_count, frame_count, height, columns, channels)
    hidden = jax.nn.silu(normed * norm_gain + norm_shift).astype(jnp.bfloat16)

    def spatial_frame(single_frame):
        padded = jnp.pad(single_frame, ((1, 1), (1, 1), (0, 0)))
        running = jnp.zeros((height * columns, channels), jnp.float32)
        for row_tap in range(3):
            for col_tap in range(3):
                window = padded[row_tap:row_tap + height, col_tap:col_tap + columns].reshape(height * columns, channels)
                running = running + jnp.dot(window, spatial_weight[row_tap, col_tap], preferred_element_type=jnp.float32)
        return (running + spatial_bias).astype(jnp.bfloat16).reshape(height, columns, channels)
    flat = hidden.reshape(clip_count * frame_count, height, columns, channels)
    spatial = lax.map(spatial_frame, flat).reshape(clip_count, frame_count, height, columns, channels)
    padded_time = jnp.pad(spatial, ((0, 0), (1, 1), (0, 0), (0, 0), (0, 0)))
    earlier = padded_time[:, :-2].reshape(clip_count * frame_count, height * columns, channels)
    current = padded_time[:, 1:-1].reshape(clip_count * frame_count, height * columns, channels)
    later = padded_time[:, 2:].reshape(clip_count * frame_count, height * columns, channels)
    inputs_flat = frames.reshape(clip_count * frame_count, height * columns, channels)

    def temporal_frame(inputs_tuple):
        first, middle, last, source = inputs_tuple
        running = jnp.dot(first, temporal_weight[0], preferred_element_type=jnp.float32)
        running = running + jnp.dot(middle, temporal_weight[1], preferred_element_type=jnp.float32)
        running = running + jnp.dot(last, temporal_weight[2], preferred_element_type=jnp.float32)
        return (source.astype(jnp.float32) + running + temporal_bias).astype(jnp.bfloat16)
    result = lax.map(temporal_frame, (earlier, current, later, inputs_flat))
    return result.reshape(clip_count, frame_count, height, columns, channels)
```

```python
import functools

import jax
import jax.numpy as jnp
from jax import lax
from jax.experimental import pallas as pl
from jax.experimental.pallas import tpu as pltpu
from jax.sharding import PartitionSpec as P

MESH = pl.DeviceIdType.MESH
GROUPS = 32
D = 640
H = 36
W = 64
HALF = D // 2
QUART = HALF // 4
R = 4
NCH = H // R
NRAW = 3
M = R * W
MEMBERS = 64 * H * W * (D // GROUPS)


def device(x, y, z, core):
    x, y, z = lax.rem(x + 4, 4), lax.rem(y + 4, 4), lax.rem(z + 4, 4)
    return lax.rem(x, 2), ((z * 4 + y) * 2 + x // 2) * 2 + core


def kernel(
    frames, gain, shift, sw, sb, tw, tb, out,
    xin, xf, sf, so, ss, hid, wts, outv,
    st, rs1, tot1, rs2,
    lsem, wsnd, wrcv, st_snd, st_rcv, raw_snd, raw_rcv, sp_snd, sp_rcv, sib_snd, sib_rcv, out_sem,
):
    dp = lax.axis_index("dp")
    tm = lax.axis_index("tm")
    core = lax.rem(tm, 2)
    xh = lax.rem(tm // 2, 2)
    y = lax.rem(tm // 4, 4)
    z = tm // 16
    x = xh * 2 + dp
    other = 1 - dp

    sibling = (dp, tm + 1 - 2 * core)
    partner = (dp, lax.rem(tm + 2 * core - 1 + 64, 64))
    valid = jnp.logical_and(tm > 0, tm < 63)
    x_to = device(x + 2 * core - 1, y, z, core)
    x_from = device(x + 1 - 2 * core, y, z, core)
    up = device(x, y + 1 - core, z + core, core)
    down = device(x, y - 1 + core, z - core, core)
    pos = y * (1 - core) + z * core
    g1 = y * 2 + core
    g2 = z * 2 + xh

    def first_group(k):
        g = lax.rem(g1 + k, 8)
        return device(x, g // 2, z, lax.rem(g, 2))

    def second_group(k):
        g = lax.rem(g2 + k, 8)
        return device(lax.rem(g, 2) * 2 + dp, y, g // 2, core)

    load_x = pltpu.make_async_copy(frames, xin, lsem.at[0])
    mine = pl.ds(pl.multiple_of(dp * HALF, 16), HALF)
    load_s = pltpu.make_async_copy(sw, wts.at[pl.ds(0, 9), mine, :], lsem.at[1])
    load_t = pltpu.make_async_copy(tw, wts.at[pl.ds(9, 3), mine, :], lsem.at[2])
    load_x.start()
    load_s.start()
    load_t.start()

    barrier = pltpu.get_barrier_semaphore()
    greet = [sibling, partner, x_to, x_from, up, down]
    greet += [first_group(k) for k in range(1, 8)] + [second_group(k) for k in range(1, 8)]
    for who in greet:
        pl.semaphore_signal(barrier, inc=1, device_id=who, device_id_type=MESH)
    pl.semaphore_wait(barrier, len(greet))

    def send(src, dst, ssem, rsem, who):
        return pltpu.make_async_remote_copy(
            src_ref=src, dst_ref=dst, send_sem=ssem, recv_sem=rsem, device_id=who, device_id_type=MESH
        )

    def part(half, owner_core, q, first=0, count=6):
        rows = pl.ds(pl.multiple_of(half * HALF + lax.rem(q + 4, 4) * QUART, 16), QUART)
        return wts.at[pl.ds(owner_core * 6 + first, count), rows, :]

    def wcopy(piece, i, who):
        return send(piece, piece, wsnd.at[i], wrcv.at[i], who)

    load_s.wait()
    load_t.wait()
    x_out = wcopy(part(dp, core, pos), 0, x_to)
    x_out.start()

    load_x.wait()

    def add_rows(i, carry):
        s, q = carry
        v = xin[pl.ds(pl.multiple_of(i * W, W), W), :].astype(jnp.float32).reshape(W // 8, 8, D)
        return s + jnp.sum(v, axis=0), q + jnp.sum(v * v, axis=0)

    zero = jnp.zeros((8, D), jnp.float32)
    s, q = lax.fori_loop(0, H, add_rows, (zero, zero))
    st[0:1, :] = jnp.sum(s, axis=0, keepdims=True)
    st[1:2, :] = jnp.sum(q, axis=0, keepdims=True)
    ones = []
    for k in range(1, 8):
        ones.append(send(st, rs1.at[k - 1], st_snd.at[k - 1], st_rcv.at[k - 1], first_group(k)))
        ones[-1].start()
    hid[0:W, :] = jnp.zeros((W, 3 * D), jnp.bfloat16)
    hid[(H + 1) * W:(H + 2) * W, :] = jnp.zeros((W, 3 * D), jnp.bfloat16)
    for c in ones:
        c.wait_recv()
    tot1[...] = st[...] + jnp.sum(rs1[...], axis=0)
    twos = []
    for k in range(1, 8):
        twos.append(send(tot1, rs2.at[k - 1], st_snd.at[k + 6], st_rcv.at[k + 6], second_group(k)))
        twos[-1].start()
    for c in twos:
        c.wait_recv()
    total = tot1[...] + jnp.sum(rs2[...], axis=0)

    ch = lax.broadcasted_iota(jnp.int32, (D, 128), 0)
    gr = lax.broadcasted_iota(jnp.int32, (D, 128), 1) * (D // GROUPS)
    member = jnp.logical_and(ch >= gr, ch < gr + D // GROUPS).astype(jnp.float32)
    ch_t = lax.broadcasted_iota(jnp.int32, (128, D), 1)
    gr_t = lax.broadcasted_iota(jnp.int32, (128, D), 0) * (D // GROUPS)
    spread = jnp.logical_and(ch_t >= gr_t, ch_t < gr_t + D // GROUPS).astype(jnp.float32)
    eight = jnp.concatenate([total, jnp.zeros((6, D), jnp.float32)], axis=0)
    per_group = jnp.dot(
        eight, member, precision=lax.Precision.HIGHEST, preferred_element_type=jnp.float32
    ) * (1.0 / MEMBERS)
    average = per_group[0:1, :]
    inv = lax.rsqrt(per_group[1:2, :] - average * average + 1e-5)
    pair = jnp.concatenate([average, inv, jnp.zeros((6, 128), jnp.float32)], axis=0)
    pair = jnp.dot(pair, spread, precision=lax.Precision.HIGHEST, preferred_element_type=jnp.float32)
    scale = pair[1:2, :] * gain[...]
    half_scale = scale * 0.5
    half_shift = (shift[...] - pair[0:1, :] * scale) * 0.5
    bias_s = sb[...]
    bias_t = tb[...]

    col = lax.broadcasted_iota(jnp.int32, (W, 128), 0)
    not_first = col > 0
    not_last = col < W - 1

    def normalise_row(src, row):
        base = pl.multiple_of(row * W, W)
        to = pl.ds(pl.multiple_of((row + 1) * W, W), W)
        for b in range(D // 128):
            lanes = slice(b * 128, (b + 1) * 128)
            v = src[pl.ds(base, W), lanes].astype(jnp.float32)
            u = v * half_scale[:, lanes] + half_shift[:, lanes]
            h = u + u * jnp.tanh(u)
            before = jnp.where(not_first, pltpu.roll(h, 1, 0), 0.0)
            after = jnp.where(not_last, pltpu.roll(h, W - 1, 0), 0.0)
            hid[to, lanes] = before.astype(jnp.bfloat16)
            hid[to, D + b * 128:D + (b + 1) * 128] = h.astype(jnp.bfloat16)
            hid[to, 2 * D + b * 128:2 * D + (b + 1) * 128] = after.astype(jnp.bfloat16)

    wcopy(part(other, core, pos), 0, x_to).wait_recv()
    theirs = 1 - core
    ring = [
        wcopy(part(other, core, pos), 1, up),
        wcopy(part(other, core, pos), 2, down),
        wcopy(part(other, core, pos), 5, sibling),
    ]
    for c in ring:
        c.start()

    pre = send(xin.at[pl.ds(0, W), :], xf.at[pl.ds(0, W), :], raw_snd.at[NRAW], raw_rcv.at[NRAW], partner)
    pre.start()

    def raw_copy(i):
        rows = pl.ds(pl.multiple_of(i * M + W, W), M)
        return send(xin.at[rows, :], xf.at[rows, :], raw_snd.at[i], raw_rcv.at[i], partner)

    def start_raw(i, _):
        raw_copy(i).start()
        return 0

    lax.fori_loop(0, NRAW, start_raw, 0)

    def own_row(i, _):
        normalise_row(xin, i)
        return 0

    lax.fori_loop(0, H // 2, own_row, 0)

    wcopy(part(other, core, pos - 1), 1, up).wait_recv()
    more = [wcopy(part(other, core, pos - 1, 0, 3), 3, up), wcopy(part(other, core, pos - 1), 6, sibling)]
    for c in more:
        c.start()
    wcopy(part(other, core, pos + 1), 2, down).wait_recv()
    more2 = [wcopy(part(other, core, pos + 1, 3, 3), 4, down), wcopy(part(other, core, pos + 1), 7, sibling)]
    for c in more2:
        c.start()

    lax.fori_loop(H // 2, H, own_row, 0)

    wcopy(part(other, core, pos + 2, 0, 3), 3, up).wait_recv()
    last = [wcopy(part(other, core, pos + 2, 0, 3), 8, sibling)]
    last[0].start()
    wcopy(part(other, core, pos + 2, 3, 3), 4, down).wait_recv()
    last.append(wcopy(part(other, core, pos + 2, 3, 3), 9, sibling))
    last[1].start()
    their_pos = y * (1 - theirs) + z * theirs
    for piece, i in (
        (part(other, theirs, their_pos), 5),
        (part(other, theirs, their_pos - 1), 6),
        (part(other, theirs, their_pos + 1), 7),
        (part(other, theirs, their_pos + 2, 0, 3), 8),
        (part(other, theirs, their_pos + 2, 3, 3), 9),
    ):
        wcopy(piece, i, sibling).wait_recv()

    def conv(i, dst):
        acc = jnp.broadcast_to(bias_s, (M, D))
        for a in range(3):
            rows = pl.ds(pl.multiple_of(i * M + a * W, W), M)
            acc = acc + jnp.dot(
                hid[rows, :], wts[3 * a:3 * a + 3].reshape(3 * D, D), preferred_element_type=jnp.float32
            )
        dst[pl.ds(pl.multiple_of(i * M, M), M), :] = acc.astype(jnp.bfloat16)

    def chunk(ref, i):
        return ref.at[pl.ds(pl.multiple_of(i * M, M), M), :]

    def to_sibling(i):
        return send(chunk(so, i), chunk(ss, i), sib_snd.at[i], sib_rcv.at[i], sibling)

    def to_partner(i):
        return send(chunk(so, i), chunk(sf, i), sp_snd.at[i], sp_rcv.at[i], partner)

    def shared_chunk(i, _):
        conv(i, so)
        to_partner(i).start()
        to_sibling(i).start()
        return 0

    lax.fori_loop(NRAW, NCH, shared_chunk, 0)

    def own_chunk(i, _):
        conv(i, so)
        to_sibling(i).start()
        return 0

    lax.fori_loop(0, NRAW, own_chunk, 0)

    far_tap = 9 + 2 * core
    near_tap = 11 - 2 * core

    def store(i):
        return pltpu.make_async_copy(chunk(outv, i), chunk(out, i), out_sem.at[i])

    def temporal(i):
        to_sibling(i).wait_recv()
        rows = pl.ds(pl.multiple_of(i * M, M), M)
        acc = xin[rows, :].astype(jnp.float32) + bias_t
        acc = acc + jnp.dot(so[rows, :], wts[10], preferred_element_type=jnp.float32)
        acc = acc + jnp.dot(ss[rows, :], wts[near_tap], preferred_element_type=jnp.float32)
        far = sf[rows, :]
        far = jnp.where(valid, far, jnp.zeros_like(far))
        acc = acc + jnp.dot(far, wts[far_tap], preferred_element_type=jnp.float32)
        outv[rows, :] = acc.astype(jnp.bfloat16)
        store(i).start()

    pre.wait_recv()
    normalise_row(xf, 0)

    def raw_chunk(i, _):
        raw_copy(i).wait_recv()

        def one(j, _):
            normalise_row(xf, i * R + 1 + j)
            return 0

        lax.fori_loop(0, R, one, 0)
        conv(i, sf)
        temporal(i)
        return 0

    lax.fori_loop(0, NRAW, raw_chunk, 0)

    def sent_chunk(i, _):
        to_partner(i).wait_recv()
        temporal(i)
        return 0

    lax.fori_loop(NRAW, NCH, sent_chunk, 0)

    for c in ones + twos + [x_out] + ring + more + more2 + last + [pre]:
        c.wait_send()

    def drain_raw(i, _):
        raw_copy(i).wait_send()
        return 0

    lax.fori_loop(0, NRAW, drain_raw, 0)

    def drain_partner(i, _):
        to_partner(i).wait_send()
        return 0

    lax.fori_loop(NRAW, NCH, drain_partner, 0)

    def drain_all(i, _):
        to_sibling(i).wait_send()
        store(i).wait()
        return 0

    lax.fori_loop(0, NCH, drain_all, 0)


def shards(frames, norm_gain, norm_shift, spatial_weight, spatial_bias, temporal_weight, temporal_bias):
    row = lambda v: v.reshape(1, D)
    vm = pl.BlockSpec(memory_space=pltpu.VMEM)
    hbm = pl.BlockSpec(memory_space=pl.ANY)
    dma = pltpu.SemaphoreType.DMA
    bf = jnp.bfloat16
    result = pl.pallas_call(
        kernel,
        out_shape=jax.ShapeDtypeStruct((H * W, D), bf),
        in_specs=[hbm, vm, vm, hbm, vm, hbm, vm],
        out_specs=hbm,
        scratch_shapes=[
            pltpu.VMEM((H * W, D), bf),
            pltpu.VMEM(((NRAW * R + 1) * W, D), bf),
            pltpu.VMEM((H * W, D), bf),
            pltpu.VMEM((H * W, D), bf),
            pltpu.VMEM((H * W, D), bf),
            pltpu.VMEM(((H + 2) * W, 3 * D), bf),
            pltpu.VMEM((12, D, D), bf),
            pltpu.VMEM((H * W, D), bf),
            pltpu.VMEM((2, D), jnp.float32),
            pltpu.VMEM((7, 2, D), jnp.float32),
            pltpu.VMEM((2, D), jnp.float32),
            pltpu.VMEM((7, 2, D), jnp.float32),
            dma((3,)), dma((10,)), dma((10,)), dma((14,)), dma((14,)),
            dma((NRAW + 1,)), dma((NRAW + 1,)), dma((NCH,)), dma((NCH,)),
            dma((NCH,)), dma((NCH,)), dma((NCH,)),
        ],
        compiler_params=pltpu.CompilerParams(
            collective_id=0, has_side_effects=True, vmem_limit_bytes=56 * 2**20
        ),
    )(
        frames.reshape(H * W, D), row(norm_gain), row(norm_shift),
        spatial_weight.reshape(9, HALF, D), row(spatial_bias), temporal_weight, row(temporal_bias),
    )
    return result.reshape(1, 1, H, W, D)


def solution(mesh):
    in_specs = (
        P("dp", "tm", None, None, None),
        P(),
        P(),
        P(None, None, "dp", None),
        P(),
        P(None, "dp", None),
        P(),
    )
    out_specs = P("dp", "tm", None, None, None)
    return jax.shard_map(shards, mesh=mesh, in_specs=in_specs, out_specs=out_specs, check_vma=False)
```

```python
import functools

import jax
import jax.numpy as jnp
from jax import lax
from jax.experimental import pallas as pl
from jax.experimental.pallas import tpu as pltpu
from jax.sharding import PartitionSpec as P

MESH = pl.DeviceIdType.MESH
GROUPS = 32
D = 640
H = 36
W = 64
HALF = D // 2
QUART = HALF // 4
R = 4
NCH = H // R
NRAW = 4
SERVE = 5
KA = 256
KB = D - KA
M = R * W
MEMBERS = 64 * H * W * (D // GROUPS)


def device(x, y, z, core):
    x, y, z = lax.rem(x + 4, 4), lax.rem(y + 4, 4), lax.rem(z + 4, 4)
    return lax.rem(x, 2), ((z * 4 + y) * 2 + x // 2) * 2 + core


def kernel(
    frames, gain, shift, sw, sb, tw, tb, out,
    xin, xf, sf, so, ss, hid, wts, outv, partial,
    st, rs1, tot1, rs2,
    lsem, wsnd, wrcv, st_snd, st_rcv, raw_snd, raw_rcv, sp_snd, sp_rcv, sib_snd, sib_rcv, out_sem,
):
    dp = lax.axis_index("dp")
    tm = lax.axis_index("tm")
    core = lax.rem(tm, 2)
    xh = lax.rem(tm // 2, 2)
    y = lax.rem(tm // 4, 4)
    z = tm // 16
    x = xh * 2 + dp
    other = 1 - dp

    sibling = (dp, tm + 1 - 2 * core)
    partner = (dp, lax.rem(tm + 2 * core - 1 + 64, 64))
    valid = jnp.logical_and(tm > 0, tm < 63)
    x_to = device(x + 2 * core - 1, y, z, core)
    x_from = device(x + 1 - 2 * core, y, z, core)
    up = device(x, y + 1 - core, z + core, core)
    down = device(x, y - 1 + core, z - core, core)
    pos = y * (1 - core) + z * core
    g1 = y * 2 + core
    g2 = z * 2 + xh

    def first_group(k):
        g = lax.rem(g1 + k, 8)
        return device(x, g // 2, z, lax.rem(g, 2))

    def second_group(k):
        g = lax.rem(g2 + k, 8)
        return device(lax.rem(g, 2) * 2 + dp, y, g // 2, core)

    load_x = pltpu.make_async_copy(frames, xin, lsem.at[0])
    mine = pl.ds(pl.multiple_of(dp * HALF, 16), HALF)
    load_s = pltpu.make_async_copy(sw, wts.at[pl.ds(0, 9), mine, :], lsem.at[1])
    load_t = pltpu.make_async_copy(tw, wts.at[pl.ds(9, 3), mine, :], lsem.at[2])
    load_x.start()
    load_s.start()
    load_t.start()

    barrier = pltpu.get_barrier_semaphore()
    greet = [sibling, partner, x_to, x_from, up, down]
    greet += [first_group(k) for k in range(1, 8)] + [second_group(k) for k in range(1, 8)]
    for who in greet:
        pl.semaphore_signal(barrier, inc=1, device_id=who, device_id_type=MESH)
    pl.semaphore_wait(barrier, len(greet))

    def send(src, dst, ssem, rsem, who):
        return pltpu.make_async_remote_copy(
            src_ref=src, dst_ref=dst, send_sem=ssem, recv_sem=rsem, device_id=who, device_id_type=MESH
        )

    def part(half, owner_core, q, first=0, count=6):
        rows = pl.ds(pl.multiple_of(half * HALF + lax.rem(q + 4, 4) * QUART, 16), QUART)
        return wts.at[pl.ds(owner_core * 6 + first, count), rows, :]

    def wcopy(piece, i, who):
        return send(piece, piece, wsnd.at[i], wrcv.at[i], who)

    load_s.wait()
    load_t.wait()
    x_out = wcopy(part(dp, core, pos), 0, x_to)
    x_out.start()

    pre = send(frames.at[pl.ds(0, W), :], xf.at[pl.ds(0, W), :], raw_snd.at[NRAW], raw_rcv.at[NRAW], partner)

    def raw_copy(i):
        rows = pl.ds(pl.multiple_of(i * M + W, W), M)
        return send(frames.at[rows, :], xf.at[rows, :], raw_snd.at[i], raw_rcv.at[i], partner)

    def start_raw(i, _):
        raw_copy(i).start()
        return 0

    load_x.wait()

    def add_rows(i, carry):
        s, q = carry
        v = xin[pl.ds(pl.multiple_of(i * W, W), W), :].astype(jnp.float32).reshape(W // 8, 8, D)
        return s + jnp.sum(v, axis=0), q + jnp.sum(v * v, axis=0)

    zero = jnp.zeros((8, D), jnp.float32)
    s, q = lax.fori_loop(0, H, add_rows, (zero, zero))
    st[0:1, :] = jnp.sum(s, axis=0, keepdims=True)
    st[1:2, :] = jnp.sum(q, axis=0, keepdims=True)
    ones = []
    for k in range(1, 8):
        ones.append(send(st, rs1.at[k - 1], st_snd.at[k - 1], st_rcv.at[k - 1], first_group(k)))
        ones[-1].start()
    hid[0:W, :] = jnp.zeros((W, 3 * D), jnp.bfloat16)
    hid[(H + 1) * W:(H + 2) * W, :] = jnp.zeros((W, 3 * D), jnp.bfloat16)
    x_out.wait_send()
    for c in ones:
        c.wait_recv()
    tot1[...] = st[...] + jnp.sum(rs1[...], axis=0)
    twos = []
    for k in range(1, 8):
        twos.append(send(tot1, rs2.at[k - 1], st_snd.at[k + 6], st_rcv.at[k + 6], second_group(k)))
        twos[-1].start()

    wcopy(part(other, core, pos), 0, x_to).wait_recv()
    theirs = 1 - core
    ring = [
        wcopy(part(other, core, pos), 1, up),
        wcopy(part(other, core, pos), 2, down),
        wcopy(part(other, core, pos), 5, sibling),
    ]
    for c in ring:
        c.start()
    pre.start()
    lax.fori_loop(0, 2, start_raw, 0)

    for c in twos:
        c.wait_recv()
    total = tot1[...] + jnp.sum(rs2[...], axis=0)

    ch = lax.broadcasted_iota(jnp.int32, (D, 128), 0)
    gr = lax.broadcasted_iota(jnp.int32, (D, 128), 1) * (D // GROUPS)
    member = jnp.logical_and(ch >= gr, ch < gr + D // GROUPS).astype(jnp.float32)
    ch_t = lax.broadcasted_iota(jnp.int32, (128, D), 1)
    gr_t = lax.broadcasted_iota(jnp.int32, (128, D), 0) * (D // GROUPS)
    spread = jnp.logical_and(ch_t >= gr_t, ch_t < gr_t + D // GROUPS).astype(jnp.float32)
    eight = jnp.concatenate([total, jnp.zeros((6, D), jnp.float32)], axis=0)
    per_group = jnp.dot(
        eight, member, precision=lax.Precision.HIGHEST, preferred_element_type=jnp.float32
    ) * (1.0 / MEMBERS)
    average = per_group[0:1, :]
    inv = lax.rsqrt(per_group[1:2, :] - average * average + 1e-5)
    pair = jnp.concatenate([average, inv, jnp.zeros((6, 128), jnp.float32)], axis=0)
    pair = jnp.dot(pair, spread, precision=lax.Precision.HIGHEST, preferred_element_type=jnp.float32)
    scale = pair[1:2, :] * gain[...].reshape(1, D)
    half_scale = scale * 0.5
    half_shift = (shift[...].reshape(1, D) - pair[0:1, :] * scale) * 0.5
    bias_s = sb[...].reshape(1, D)
    bias_t = tb[...].reshape(1, D)

    col = lax.broadcasted_iota(jnp.int32, (W, 128), 0)
    not_first = col > 0
    not_last = col < W - 1

    def normalise_row(src, row):
        base = pl.multiple_of(row * W, W)
        to = pl.ds(pl.multiple_of((row + 1) * W, W), W)
        for b in range(D // 128):
            lanes = slice(b * 128, (b + 1) * 128)
            v = src[pl.ds(base, W), lanes].astype(jnp.float32)
            u = v * half_scale[:, lanes] + half_shift[:, lanes]
            h = u + u * jnp.tanh(u)
            before = jnp.where(not_first, pltpu.roll(h, 1, 0), 0.0)
            after = jnp.where(not_last, pltpu.roll(h, W - 1, 0), 0.0)
            hid[to, lanes] = before.astype(jnp.bfloat16)
            hid[to, D + b * 128:D + (b + 1) * 128] = h.astype(jnp.bfloat16)
            hid[to, 2 * D + b * 128:2 * D + (b + 1) * 128] = after.astype(jnp.bfloat16)

    def own_row(i, _):
        normalise_row(xin, i)
        return 0

    lax.fori_loop(0, H, own_row, 0)

    first_ka = pl.multiple_of(dp * KB, 128)
    first_kb = pl.multiple_of((1 - dp) * KA, 128)

    def taps(i, start, count):
        left = []
        for a in range(3):
            rows = pl.ds(pl.multiple_of(i * M + a * W, W), M)
            for b in range(3):
                left.append(hid[rows, pl.ds(pl.multiple_of(b * D + start, 128), count)])
        left = jnp.concatenate(left, axis=1)
        right = wts[0:9, pl.ds(start, count), :].reshape(9 * count, D)
        return jnp.dot(left, right, preferred_element_type=jnp.float32)

    def conv_a(i, _):
        partial[pl.ds(pl.multiple_of(i * M, M), M), :] = taps(i, first_ka, KA)
        return 0

    def conv_b(i):
        rows = pl.ds(pl.multiple_of(i * M, M), M)
        acc = partial[rows, :] + bias_s + taps(i, first_kb, KB)
        so[rows, :] = acc.astype(jnp.bfloat16)

    lax.fori_loop(0, SERVE, conv_a, 0)

    wcopy(part(other, core, pos - 1), 1, up).wait_recv()
    more = [wcopy(part(other, core, pos - 1, 0, 3), 3, up), wcopy(part(other, core, pos - 1), 6, sibling)]
    for c in more:
        c.start()
    wcopy(part(other, core, pos + 1), 2, down).wait_recv()
    more2 = [wcopy(part(other, core, pos + 1, 3, 3), 4, down), wcopy(part(other, core, pos + 1), 7, sibling)]
    for c in more2:
        c.start()
    lax.fori_loop(2, NRAW, start_raw, 0)

    lax.fori_loop(SERVE, NCH, conv_a, 0)

    wcopy(part(other, core, pos + 2, 0, 3), 3, up).wait_recv()
    last = [wcopy(part(other, core, pos + 2, 0, 3), 8, sibling)]
    last[0].start()
    wcopy(part(other, core, pos + 2, 3, 3), 4, down).wait_recv()
    last.append(wcopy(part(other, core, pos + 2, 3, 3), 9, sibling))
    last[1].start()
    their_pos = y * (1 - theirs) + z * theirs
    for piece, i in (
        (part(other, theirs, their_pos), 5),
        (part(other, theirs, their_pos - 1), 6),
        (part(other, theirs, their_pos + 1), 7),
        (part(other, theirs, their_pos + 2, 0, 3), 8),
        (part(other, theirs, their_pos + 2, 3, 3), 9),
    ):
        wcopy(piece, i, sibling).wait_recv()

    def conv_far(i):
        acc = taps(i, 0, D) + bias_s
        sf[pl.ds(pl.multiple_of(i * M, M), M), :] = acc.astype(jnp.bfloat16)

    def chunk(ref, i):
        return ref.at[pl.ds(pl.multiple_of(i * M, M), M), :]

    def to_sibling(i):
        return send(chunk(so, i), chunk(ss, i), sib_snd.at[i], sib_rcv.at[i], sibling)

    def to_partner(i):
        return send(chunk(so, i), chunk(sf, i), sp_snd.at[i], sp_rcv.at[i], partner)

    def shared_chunk(i, _):
        conv_b(i)
        to_partner(i).start()
        to_sibling(i).start()
        return 0

    lax.fori_loop(NRAW, NCH, shared_chunk, 0)

    def own_chunk(i, _):
        conv_b(i)
        to_sibling(i).start()
        return 0

    lax.fori_loop(0, NRAW, own_chunk, 0)

    far_tap = 9 + 2 * core
    near_tap = 11 - 2 * core

    def store(i):
        return pltpu.make_async_copy(chunk(outv, i), chunk(out, i), out_sem.at[i])

    def temporal(i):
        to_sibling(i).wait_recv()
        rows = pl.ds(pl.multiple_of(i * M, M), M)
        acc = xin[rows, :].astype(jnp.float32) + bias_t
        acc = acc + jnp.dot(so[rows, :], wts[10], preferred_element_type=jnp.float32)
        acc = acc + jnp.dot(ss[rows, :], wts[near_tap], preferred_element_type=jnp.float32)
        far = sf[rows, :]
        far = jnp.where(valid, far, jnp.zeros_like(far))
        acc = acc + jnp.dot(far, wts[far_tap], preferred_element_type=jnp.float32)
        outv[rows, :] = acc.astype(jnp.bfloat16)
        store(i).start()

    pre.wait_recv()
    normalise_row(xf, 0)

    def raw_chunk(i, _):
        raw_copy(i).wait_recv()

        def one(j, _):
            normalise_row(xf, i * R + 1 + j)
            return 0

        lax.fori_loop(0, R, one, 0)
        conv_far(i)
        temporal(i)
        return 0

    lax.fori_loop(0, NRAW, raw_chunk, 0)

    def sent_chunk(i, _):
        to_partner(i).wait_recv()
        temporal(i)
        return 0

    lax.fori_loop(NRAW, NCH, sent_chunk, 0)

    for c in ones + twos + ring + more + more2 + last + [pre]:
        c.wait_send()

    def drain_raw(i, _):
        raw_copy(i).wait_send()
        return 0

    lax.fori_loop(0, NRAW, drain_raw, 0)

    def drain_partner(i, _):
        to_partner(i).wait_send()
        return 0

    lax.fori_loop(NRAW, NCH, drain_partner, 0)

    def drain_all(i, _):
        to_sibling(i).wait_send()
        store(i).wait()
        return 0

    lax.fori_loop(0, NCH, drain_all, 0)


def shards(frames, norm_gain, norm_shift, spatial_weight, spatial_bias, temporal_weight, temporal_bias):
    vm = pl.BlockSpec(memory_space=pltpu.VMEM)
    hbm = pl.BlockSpec(memory_space=pl.ANY)
    dma = pltpu.SemaphoreType.DMA
    bf = jnp.bfloat16
    result = pl.pallas_call(
        kernel,
        out_shape=jax.ShapeDtypeStruct((H * W, D), bf),
        in_specs=[hbm, vm, vm, hbm, vm, hbm, vm],
        out_specs=hbm,
        scratch_shapes=[
            pltpu.VMEM((H * W, D), bf),
            pltpu.VMEM(((NRAW * R + 1) * W, D), bf),
            pltpu.VMEM((H * W, D), bf),
            pltpu.VMEM((H * W, D), bf),
            pltpu.VMEM((H * W, D), bf),
            pltpu.VMEM(((H + 2) * W, 3 * D), bf),
            pltpu.VMEM((12, D, D), bf),
            pltpu.VMEM((H * W, D), bf),
            pltpu.VMEM((H * W, D), jnp.float32),
            pltpu.VMEM((2, D), jnp.float32),
            pltpu.VMEM((7, 2, D), jnp.float32),
            pltpu.VMEM((2, D), jnp.float32),
            pltpu.VMEM((7, 2, D), jnp.float32),
            dma((3,)), dma((10,)), dma((10,)), dma((14,)), dma((14,)),
            dma((NRAW + 1,)), dma((NRAW + 1,)), dma((NCH,)), dma((NCH,)),
            dma((NCH,)), dma((NCH,)), dma((NCH,)),
        ],
        compiler_params=pltpu.CompilerParams(
            collective_id=0, has_side_effects=True, vmem_limit_bytes=56 * 2**20
        ),
    )(
        frames.reshape(H * W, D), norm_gain, norm_shift,
        spatial_weight.reshape(9, HALF, D), spatial_bias, temporal_weight, temporal_bias,
    )
    return result.reshape(1, 1, H, W, D)


def solution(mesh):
    in_specs = (
        P("dp", "tm", None, None, None),
        P(),
        P(),
        P(None, None, "dp", None),
        P(),
        P(None, "dp", None),
        P(),
    )
    out_specs = P("dp", "tm", None, None, None)
    return jax.shard_map(shards, mesh=mesh, in_specs=in_specs, out_specs=out_specs, check_vma=False)
```

```python
import functools

import jax
import jax.numpy as jnp
from jax import lax
from jax.experimental import pallas as pl
from jax.experimental.pallas import tpu as pltpu
from jax.sharding import PartitionSpec as P

MESH = pl.DeviceIdType.MESH
GROUPS = 32
D = 640
H = 36
W = 64
HALF = D // 2
QUART = HALF // 4
R = 4
NCH = H // R
NRAW = 4
SERVE = 5
KA = 256
KB = D - KA
M = R * W
MEMBERS = 64 * H * W * (D // GROUPS)


def device(x, y, z, core):
    x, y, z = lax.rem(x + 4, 4), lax.rem(y + 4, 4), lax.rem(z + 4, 4)
    return lax.rem(x, 2), ((z * 4 + y) * 2 + x // 2) * 2 + core


def kernel(
    frames, gain, shift, sw, sb, tw, tb, out,
    xin, xf, sf, so, ss, hid, wts, partial,
    st, rs1, tot1, rs2,
    lsem, wsnd, wrcv, st_snd, st_rcv, raw_snd, raw_rcv, sp_snd, sp_rcv, sib_snd, sib_rcv,
):
    dp = lax.axis_index("dp")
    tm = lax.axis_index("tm")
    core = lax.rem(tm, 2)
    xh = lax.rem(tm // 2, 2)
    y = lax.rem(tm // 4, 4)
    z = tm // 16
    x = xh * 2 + dp
    other = 1 - dp

    sibling = (dp, tm + 1 - 2 * core)
    partner = (dp, lax.rem(tm + 2 * core - 1 + 64, 64))
    valid = jnp.logical_and(tm > 0, tm < 63)
    x_to = device(x + 2 * core - 1, y, z, core)
    x_from = device(x + 1 - 2 * core, y, z, core)
    up = device(x, y + 1 - core, z + core, core)
    down = device(x, y - 1 + core, z - core, core)
    pos = y * (1 - core) + z * core
    g1 = y * 2 + core
    g2 = z * 2 + xh

    def first_group(k):
        g = lax.rem(g1 + k, 8)
        return device(x, g // 2, z, lax.rem(g, 2))

    def second_group(k):
        g = lax.rem(g2 + k, 8)
        return device(lax.rem(g, 2) * 2 + dp, y, g // 2, core)

    load_x = pltpu.make_async_copy(frames, xin, lsem.at[0])
    mine = pl.ds(pl.multiple_of(dp * HALF, 16), HALF)
    load_s = pltpu.make_async_copy(sw, wts.at[pl.ds(0, 9), mine, :], lsem.at[1])
    load_t = pltpu.make_async_copy(tw, wts.at[pl.ds(9, 3), mine, :], lsem.at[2])
    load_x.start()
    load_s.start()
    load_t.start()

    barrier = pltpu.get_barrier_semaphore()
    greet = [sibling, partner, x_to, x_from, up, down]
    greet += [first_group(k) for k in range(1, 8)] + [second_group(k) for k in range(1, 8)]
    for who in greet:
        pl.semaphore_signal(barrier, inc=1, device_id=who, device_id_type=MESH)
    pl.semaphore_wait(barrier, len(greet))

    def send(src, dst, ssem, rsem, who):
        return pltpu.make_async_remote_copy(
            src_ref=src, dst_ref=dst, send_sem=ssem, recv_sem=rsem, device_id=who, device_id_type=MESH
        )

    def part(half, owner_core, q, first=0, count=6):
        rows = pl.ds(pl.multiple_of(half * HALF + lax.rem(q + 4, 4) * QUART, 16), QUART)
        return wts.at[pl.ds(owner_core * 6 + first, count), rows, :]

    def wcopy(piece, i, who):
        return send(piece, piece, wsnd.at[i], wrcv.at[i], who)

    load_s.wait()
    load_t.wait()
    x_out = wcopy(part(dp, core, pos), 0, x_to)
    x_out.start()

    pre = send(frames.at[pl.ds(0, W), :], xf.at[pl.ds(0, W), :], raw_snd.at[NRAW], raw_rcv.at[NRAW], partner)

    def raw_copy(i):
        rows = pl.ds(pl.multiple_of(i * M + W, W), M)
        return send(frames.at[rows, :], xf.at[rows, :], raw_snd.at[i], raw_rcv.at[i], partner)

    def start_raw(i, _):
        raw_copy(i).start()
        return 0

    load_x.wait()

    def add_rows(i, carry):
        s, q = carry
        v = xin[pl.ds(pl.multiple_of(i * W, W), W), :].astype(jnp.float32).reshape(W // 8, 8, D)
        return s + jnp.sum(v, axis=0), q + jnp.sum(v * v, axis=0)

    zero = jnp.zeros((8, D), jnp.float32)
    s, q = lax.fori_loop(0, H, add_rows, (zero, zero))
    st[0:1, :] = jnp.sum(s, axis=0, keepdims=True)
    st[1:2, :] = jnp.sum(q, axis=0, keepdims=True)
    ones = []
    for k in range(1, 8):
        ones.append(send(st, rs1.at[k - 1], st_snd.at[k - 1], st_rcv.at[k - 1], first_group(k)))
        ones[-1].start()
    hid[0:W, :] = jnp.zeros((W, 3 * D), jnp.bfloat16)
    hid[(H + 1) * W:(H + 2) * W, :] = jnp.zeros((W, 3 * D), jnp.bfloat16)
    x_out.wait_send()
    for c in ones:
        c.wait_recv()
    tot1[...] = st[...] + jnp.sum(rs1[...], axis=0)
    twos = []
    for k in range(1, 8):
        twos.append(send(tot1, rs2.at[k - 1], st_snd.at[k + 6], st_rcv.at[k + 6], second_group(k)))
        twos[-1].start()

    wcopy(part(other, core, pos), 0, x_to).wait_recv()
    theirs = 1 - core
    ring = [
        wcopy(part(other, core, pos), 1, up),
        wcopy(part(other, core, pos), 2, down),
        wcopy(part(other, core, pos), 5, sibling),
    ]
    for c in ring:
        c.start()
    pre.start()
    lax.fori_loop(0, 2, start_raw, 0)

    for c in twos:
        c.wait_recv()
    total = tot1[...] + jnp.sum(rs2[...], axis=0)

    ch = lax.broadcasted_iota(jnp.int32, (D, 128), 0)
    gr = lax.broadcasted_iota(jnp.int32, (D, 128), 1) * (D // GROUPS)
    member = jnp.logical_and(ch >= gr, ch < gr + D // GROUPS).astype(jnp.float32)
    ch_t = lax.broadcasted_iota(jnp.int32, (128, D), 1)
    gr_t = lax.broadcasted_iota(jnp.int32, (128, D), 0) * (D // GROUPS)
    spread = jnp.logical_and(ch_t >= gr_t, ch_t < gr_t + D // GROUPS).astype(jnp.float32)
    eight = jnp.concatenate([total, jnp.zeros((6, D), jnp.float32)], axis=0)
    per_group = jnp.dot(
        eight, member, precision=lax.Precision.HIGHEST, preferred_element_type=jnp.float32
    ) * (1.0 / MEMBERS)
    average = per_group[0:1, :]
    inv = lax.rsqrt(per_group[1:2, :] - average * average + 1e-5)
    pair = jnp.concatenate([average, inv, jnp.zeros((6, 128), jnp.float32)], axis=0)
    pair = jnp.dot(pair, spread, precision=lax.Precision.HIGHEST, preferred_element_type=jnp.float32)
    scale = pair[1:2, :] * gain[...].reshape(1, D)
    half_scale = scale * 0.5
    half_shift = (shift[...].reshape(1, D) - pair[0:1, :] * scale) * 0.5
    bias_s = sb[...].reshape(1, D)
    bias_t = tb[...].reshape(1, D)

    col = lax.broadcasted_iota(jnp.int32, (W, 128), 0)
    not_first = col > 0
    not_last = col < W - 1

    def normalise_row(src, row):
        base = pl.multiple_of(row * W, W)
        to = pl.ds(pl.multiple_of((row + 1) * W, W), W)
        for b in range(D // 128):
            lanes = slice(b * 128, (b + 1) * 128)
            v = src[pl.ds(base, W), lanes].astype(jnp.float32)
            u = v * half_scale[:, lanes] + half_shift[:, lanes]
            h = u + u * jnp.tanh(u)
            before = jnp.where(not_first, pltpu.roll(h, 1, 0), 0.0)
            after = jnp.where(not_last, pltpu.roll(h, W - 1, 0), 0.0)
            hid[to, lanes] = before.astype(jnp.bfloat16)
            hid[to, D + b * 128:D + (b + 1) * 128] = h.astype(jnp.bfloat16)
            hid[to, 2 * D + b * 128:2 * D + (b + 1) * 128] = after.astype(jnp.bfloat16)

    def own_row(i, _):
        normalise_row(xin, i)
        return 0

    lax.fori_loop(0, H, own_row, 0)

    first_ka = pl.multiple_of(dp * KB, 128)
    first_kb = pl.multiple_of((1 - dp) * KA, 128)

    def taps(i, start, count):
        left = []
        for a in range(3):
            rows = pl.ds(pl.multiple_of(i * M + a * W, W), M)
            for b in range(3):
                left.append(hid[rows, pl.ds(pl.multiple_of(b * D + start, 128), count)])
        left = jnp.concatenate(left, axis=1)
        right = wts[0:9, pl.ds(start, count), :].reshape(9 * count, D)
        return jnp.dot(left, right, preferred_element_type=jnp.float32)

    def conv_a(i, _):
        partial[pl.ds(pl.multiple_of(i * M, M), M), :] = taps(i, first_ka, KA)
        return 0

    def conv_b(i):
        rows = pl.ds(pl.multiple_of(i * M, M), M)
        acc = partial[rows, :] + bias_s + taps(i, first_kb, KB)
        so[rows, :] = acc.astype(jnp.bfloat16)

    lax.fori_loop(0, SERVE, conv_a, 0)

    wcopy(part(other, core, pos - 1), 1, up).wait_recv()
    more = [wcopy(part(other, core, pos - 1, 0, 3), 3, up), wcopy(part(other, core, pos - 1), 6, sibling)]
    for c in more:
        c.start()
    wcopy(part(other, core, pos + 1), 2, down).wait_recv()
    more2 = [wcopy(part(other, core, pos + 1, 3, 3), 4, down), wcopy(part(other, core, pos + 1), 7, sibling)]
    for c in more2:
        c.start()
    lax.fori_loop(2, NRAW, start_raw, 0)

    lax.fori_loop(SERVE, NCH, conv_a, 0)

    wcopy(part(other, core, pos + 2, 0, 3), 3, up).wait_recv()
    last = [wcopy(part(other, core, pos + 2, 0, 3), 8, sibling)]
    last[0].start()
    wcopy(part(other, core, pos + 2, 3, 3), 4, down).wait_recv()
    last.append(wcopy(part(other, core, pos + 2, 3, 3), 9, sibling))
    last[1].start()
    their_pos = y * (1 - theirs) + z * theirs
    for piece, i in (
        (part(other, theirs, their_pos), 5),
        (part(other, theirs, their_pos - 1), 6),
        (part(other, theirs, their_pos + 1), 7),
        (part(other, theirs, their_pos + 2, 0, 3), 8),
        (part(other, theirs, their_pos + 2, 3, 3), 9),
    ):
        wcopy(piece, i, sibling).wait_recv()

    def conv_far(i):
        acc = taps(i, 0, D) + bias_s
        sf[pl.ds(pl.multiple_of(i * M, M), M), :] = acc.astype(jnp.bfloat16)

    def chunk(ref, i):
        return ref.at[pl.ds(pl.multiple_of(i * M, M), M), :]

    def to_sibling(i):
        return send(chunk(so, i), chunk(ss, i), sib_snd.at[i], sib_rcv.at[i], sibling)

    def to_partner(i):
        return send(chunk(so, i), chunk(sf, i), sp_snd.at[i], sp_rcv.at[i], partner)

    def shared_chunk(i, _):
        conv_b(i)
        to_partner(i).start()
        to_sibling(i).start()
        return 0

    lax.fori_loop(NRAW, NCH, shared_chunk, 0)

    def own_chunk(i, _):
        conv_b(i)
        to_sibling(i).start()
        return 0

    lax.fori_loop(0, NRAW, own_chunk, 0)

    far_tap = 9 + 2 * core
    near_tap = 11 - 2 * core

    def temporal(i):
        to_sibling(i).wait_recv()
        rows = pl.ds(pl.multiple_of(i * M, M), M)
        acc = xin[rows, :].astype(jnp.float32) + bias_t
        acc = acc + jnp.dot(so[rows, :], wts[10], preferred_element_type=jnp.float32)
        acc = acc + jnp.dot(ss[rows, :], wts[near_tap], preferred_element_type=jnp.float32)
        far = sf[rows, :]
        far = jnp.where(valid, far, jnp.zeros_like(far))
        acc = acc + jnp.dot(far, wts[far_tap], preferred_element_type=jnp.float32)
        out[rows, :] = acc.astype(jnp.bfloat16)

    pre.wait_recv()
    normalise_row(xf, 0)

    def raw_chunk(i, _):
        raw_copy(i).wait_recv()

        def one(j, _):
            normalise_row(xf, i * R + 1 + j)
            return 0

        lax.fori_loop(0, R, one, 0)
        conv_far(i)
        temporal(i)
        return 0

    lax.fori_loop(0, NRAW, raw_chunk, 0)

    def sent_chunk(i, _):
        to_partner(i).wait_recv()
        temporal(i)
        return 0

    lax.fori_loop(NRAW, NCH, sent_chunk, 0)

    for c in ones + twos + ring + more + more2 + last + [pre]:
        c.wait_send()

    def drain_raw(i, _):
        raw_copy(i).wait_send()
        return 0

    lax.fori_loop(0, NRAW, drain_raw, 0)

    def drain_partner(i, _):
        to_partner(i).wait_send()
        return 0

    lax.fori_loop(NRAW, NCH, drain_partner, 0)

    def drain_all(i, _):
        to_sibling(i).wait_send()
        return 0

    lax.fori_loop(0, NCH, drain_all, 0)


def shards(frames, norm_gain, norm_shift, spatial_weight, spatial_bias, temporal_weight, temporal_bias):
    vm = pl.BlockSpec(memory_space=pltpu.VMEM)
    hbm = pl.BlockSpec(memory_space=pl.ANY)
    dma = pltpu.SemaphoreType.DMA
    bf = jnp.bfloat16
    result = pl.pallas_call(
        kernel,
        out_shape=pltpu.VMEM((H * W, D), bf),
        in_specs=[hbm, vm, vm, hbm, vm, hbm, vm],
        out_specs=vm,
        scratch_shapes=[
            pltpu.VMEM((H * W, D), bf),
            pltpu.VMEM(((NRAW * R + 1) * W, D), bf),
            pltpu.VMEM((H * W, D), bf),
            pltpu.VMEM((H * W, D), bf),
            pltpu.VMEM((H * W, D), bf),
            pltpu.VMEM(((H + 2) * W, 3 * D), bf),
            pltpu.VMEM((12, D, D), bf),
            pltpu.VMEM((H * W, D), jnp.float32),
            pltpu.VMEM((2, D), jnp.float32),
            pltpu.VMEM((7, 2, D), jnp.float32),
            pltpu.VMEM((2, D), jnp.float32),
            pltpu.VMEM((7, 2, D), jnp.float32),
            dma((3,)), dma((10,)), dma((10,)), dma((14,)), dma((14,)),
            dma((NRAW + 1,)), dma((NRAW + 1,)), dma((NCH,)), dma((NCH,)),
            dma((NCH,)), dma((NCH,)),
        ],
        compiler_params=pltpu.CompilerParams(
            collective_id=0, has_side_effects=True, vmem_limit_bytes=56 * 2**20
        ),
    )(
        frames.reshape(H * W, D), norm_gain, norm_shift,
        spatial_weight.reshape(9, HALF, D), spatial_bias, temporal_weight, temporal_bias,
    )
    return result.reshape(1, 1, H, W, D)


def solution(mesh):
    in_specs = (
        P("dp", "tm", None, None, None),
        P(),
        P(),
        P(None, None, "dp", None),
        P(),
        P(None, "dp", None),
        P(),
    )
    out_specs = P("dp", "tm", None, None, None)
    return jax.shard_map(shards, mesh=mesh, in_specs=in_specs, out_specs=out_specs, check_vma=False)
```

```python
import functools

import jax
import jax.numpy as jnp
from jax import lax
from jax.experimental import pallas as pl
from jax.experimental.pallas import tpu as pltpu
from jax.sharding import PartitionSpec as P

MESH = pl.DeviceIdType.MESH
GROUPS = 32
D = 640
H = 36
W = 64
HALF = D // 2
QUART = HALF // 4
R = 4
NCH = H // R
NRAW = 4
BURST = 2
NSUB = 3
KA = 256
KB = D - KA
M = R * W
MEMBERS = 64 * H * W * (D // GROUPS)


def device(x, y, z, core):
    x, y, z = lax.rem(x + 4, 4), lax.rem(y + 4, 4), lax.rem(z + 4, 4)
    return lax.rem(x, 2), ((z * 4 + y) * 2 + x // 2) * 2 + core


def kernel(
    frames, gain, shift, sw, sb, tw, tb, out,
    xin, xf, sf, so, ss, hid, wts, partial,
    st, rs1, tot1, rs2,
    lsem, wsnd, wrcv, st_snd, st_rcv, raw_snd, raw_rcv, sp_snd, sp_rcv, sib_snd, sib_rcv,
):
    dp = lax.axis_index("dp")
    tm = lax.axis_index("tm")
    core = lax.rem(tm, 2)
    xh = lax.rem(tm // 2, 2)
    y = lax.rem(tm // 4, 4)
    z = tm // 16
    x = xh * 2 + dp
    other = 1 - dp

    sibling = (dp, tm + 1 - 2 * core)
    partner = (dp, lax.rem(tm + 2 * core - 1 + 64, 64))
    valid = jnp.logical_and(tm > 0, tm < 63)
    x_to = device(x + 2 * core - 1, y, z, core)
    x_from = device(x + 1 - 2 * core, y, z, core)
    up = device(x, y + 1 - core, z + core, core)
    down = device(x, y - 1 + core, z - core, core)
    pos = y * (1 - core) + z * core
    g1 = y * 2 + core
    g2 = z * 2 + xh

    def first_group(k):
        g = lax.rem(g1 + k, 8)
        return device(x, g // 2, z, lax.rem(g, 2))

    def second_group(k):
        g = lax.rem(g2 + k, 8)
        return device(lax.rem(g, 2) * 2 + dp, y, g // 2, core)

    load_x = pltpu.make_async_copy(frames, xin, lsem.at[0])
    mine = pl.ds(pl.multiple_of(dp * HALF, 16), HALF)
    load_s = pltpu.make_async_copy(sw, wts.at[pl.ds(0, 9), mine, :], lsem.at[1])
    load_t = pltpu.make_async_copy(tw, wts.at[pl.ds(9, 3), mine, :], lsem.at[2])
    load_x.start()
    load_s.start()
    load_t.start()

    barrier = pltpu.get_barrier_semaphore()
    greet = [sibling, partner, x_to, x_from, up, down]
    greet += [first_group(k) for k in range(1, 8)] + [second_group(k) for k in range(1, 8)]
    for who in greet:
        pl.semaphore_signal(barrier, inc=1, device_id=who, device_id_type=MESH)
    pl.semaphore_wait(barrier, len(greet))

    def send(src, dst, ssem, rsem, who):
        return pltpu.make_async_remote_copy(
            src_ref=src, dst_ref=dst, send_sem=ssem, recv_sem=rsem, device_id=who, device_id_type=MESH
        )

    def part(half, owner_core, q, first, count):
        rows = pl.ds(pl.multiple_of(half * HALF + lax.rem(q + 4, 4) * QUART, 16), QUART)
        return wts.at[pl.ds(owner_core * 6 + first, count), rows, :]

    def wcopy(piece, k, i, who):
        return send(piece, piece, wsnd.at[k, i], wrcv.at[k, i], who)

    sent = []

    def go(copy):
        copy.start()
        sent.append(copy)

    def weights_x(k):
        go(wcopy(part(dp, core, pos, 2 * k, 2), k, 0, x_to))

    def weights_ring(k):
        piece = part(other, core, pos, 2 * k, 2)
        wcopy(piece, k, 0, x_to).wait_recv()
        go(wcopy(piece, k, 1, up))
        go(wcopy(piece, k, 2, down))
        go(wcopy(piece, k, 5, sibling))

    def weights_on(k):
        piece = part(other, core, pos - 1, 2 * k, 2)
        wcopy(piece, k, 1, up).wait_recv()
        go(wcopy(part(other, core, pos - 1, 2 * k, 1), k, 3, up))
        go(wcopy(piece, k, 6, sibling))
        piece = part(other, core, pos + 1, 2 * k, 2)
        wcopy(piece, k, 2, down).wait_recv()
        go(wcopy(part(other, core, pos + 1, 2 * k + 1, 1), k, 4, down))
        go(wcopy(piece, k, 7, sibling))

    def weights_last(k):
        piece = part(other, core, pos + 2, 2 * k, 1)
        wcopy(piece, k, 3, up).wait_recv()
        go(wcopy(piece, k, 8, sibling))
        piece = part(other, core, pos + 2, 2 * k + 1, 1)
        wcopy(piece, k, 4, down).wait_recv()
        go(wcopy(piece, k, 9, sibling))

    def weights_near(k):
        theirs = 1 - core
        their_pos = y * (1 - theirs) + z * theirs
        for i, (shift_by, first, count) in enumerate((
            (0, 2 * k, 2), (-1, 2 * k, 2), (1, 2 * k, 2), (2, 2 * k, 1), (2, 2 * k + 1, 1),
        )):
            wcopy(part(other, theirs, their_pos + shift_by, first, count), k, 5 + i, sibling).wait_recv()

    load_s.wait()
    load_t.wait()
    for k in range(NSUB):
        weights_x(k)

    pre = send(frames.at[pl.ds(0, W), :], xf.at[pl.ds(0, W), :], raw_snd.at[NRAW], raw_rcv.at[NRAW], partner)

    def raw_copy(i):
        rows = pl.ds(pl.multiple_of(i * M + W, W), M)
        return send(frames.at[rows, :], xf.at[rows, :], raw_snd.at[i], raw_rcv.at[i], partner)

    def start_raw(i, _):
        raw_copy(i).start()
        return 0

    load_x.wait()

    def add_rows(i, carry):
        s, q = carry
        v = xin[pl.ds(pl.multiple_of(i * W, W), W), :].astype(jnp.float32).reshape(W // 8, 8, D)
        return s + jnp.sum(v, axis=0), q + jnp.sum(v * v, axis=0)

    zero = jnp.zeros((8, D), jnp.float32)
    s, q = lax.fori_loop(0, H, add_rows, (zero, zero))
    st[0:1, :] = jnp.sum(s, axis=0, keepdims=True)
    st[1:2, :] = jnp.sum(q, axis=0, keepdims=True)
    ones = []
    for k in range(1, 8):
        ones.append(send(st, rs1.at[k - 1], st_snd.at[k - 1], st_rcv.at[k - 1], first_group(k)))
        ones[-1].start()
    hid[0:W, :] = jnp.zeros((W, 3 * D), jnp.bfloat16)
    hid[(H + 1) * W:(H + 2) * W, :] = jnp.zeros((W, 3 * D), jnp.bfloat16)
    weights_ring(0)
    for c in ones:
        c.wait_recv()
    tot1[...] = st[...] + jnp.sum(rs1[...], axis=0)
    twos = []
    for k in range(1, 8):
        twos.append(send(tot1, rs2.at[k - 1], st_snd.at[k + 6], st_rcv.at[k + 6], second_group(k)))
        twos[-1].start()

    weights_ring(1)
    for c in twos:
        c.wait_recv()
    pre.start()
    lax.fori_loop(0, BURST, start_raw, 0)
    weights_ring(2)
    total = tot1[...] + jnp.sum(rs2[...], axis=0)

    ch = lax.broadcasted_iota(jnp.int32, (D, 128), 0)
    gr = lax.broadcasted_iota(jnp.int32, (D, 128), 1) * (D // GROUPS)
    member = jnp.logical_and(ch >= gr, ch < gr + D // GROUPS).astype(jnp.float32)
    ch_t = lax.broadcasted_iota(jnp.int32, (128, D), 1)
    gr_t = lax.broadcasted_iota(jnp.int32, (128, D), 0) * (D // GROUPS)
    spread = jnp.logical_and(ch_t >= gr_t, ch_t < gr_t + D // GROUPS).astype(jnp.float32)
    eight = jnp.concatenate([total, jnp.zeros((6, D), jnp.float32)], axis=0)
    per_group = jnp.dot(
        eight, member, precision=lax.Precision.HIGHEST, preferred_element_type=jnp.float32
    ) * (1.0 / MEMBERS)
    average = per_group[0:1, :]
    inv = lax.rsqrt(per_group[1:2, :] - average * average + 1e-5)
    pair = jnp.concatenate([average, inv, jnp.zeros((6, 128), jnp.float32)], axis=0)
    pair = jnp.dot(pair, spread, precision=lax.Precision.HIGHEST, preferred_element_type=jnp.float32)
    scale = pair[1:2, :] * gain[...].reshape(1, D)
    half_scale = scale * 0.5
    half_shift = (shift[...].reshape(1, D) - pair[0:1, :] * scale) * 0.5
    bias_s = sb[...].reshape(1, D)
    bias_t = tb[...].reshape(1, D)

    col = lax.broadcasted_iota(jnp.int32, (W, 128), 0)
    not_first = col > 0
    not_last = col < W - 1

    def normalise_row(src, row):
        base = pl.multiple_of(row * W, W)
        to = pl.ds(pl.multiple_of((row + 1) * W, W), W)
        for b in range(D // 128):
            lanes = slice(b * 128, (b + 1) * 128)
            v = src[pl.ds(base, W), lanes].astype(jnp.float32)
            u = v * half_scale[:, lanes] + half_shift[:, lanes]
            h = u + u * jnp.tanh(u)
            before = jnp.where(not_first, pltpu.roll(h, 1, 0), 0.0)
            after = jnp.where(not_last, pltpu.roll(h, W - 1, 0), 0.0)
            hid[to, lanes] = before.astype(jnp.bfloat16)
            hid[to, D + b * 128:D + (b + 1) * 128] = h.astype(jnp.bfloat16)
            hid[to, 2 * D + b * 128:2 * D + (b + 1) * 128] = after.astype(jnp.bfloat16)

    def own_row(i, _):
        normalise_row(xin, i)
        return 0

    lax.fori_loop(0, H // 2, own_row, 0)
    weights_on(0)
    lax.fori_loop(H // 2, H, own_row, 0)
    weights_on(1)

    first_ka = pl.multiple_of(dp * KB, 128)
    first_kb = pl.multiple_of((1 - dp) * KA, 128)

    def taps(i, start, count):
        left = []
        for a in range(3):
            rows = pl.ds(pl.multiple_of(i * M + a * W, W), M)
            for b in range(3):
                left.append(hid[rows, pl.ds(pl.multiple_of(b * D + start, 128), count)])
        left = jnp.concatenate(left, axis=1)
        right = wts[0:9, pl.ds(start, count), :].reshape(9 * count, D)
        return jnp.dot(left, right, preferred_element_type=jnp.float32)

    def conv_a(i, _):
        partial[pl.ds(pl.multiple_of(i * M, M), M), :] = taps(i, first_ka, KA)
        return 0

    def conv_b(i):
        rows = pl.ds(pl.multiple_of(i * M, M), M)
        acc = partial[rows, :] + bias_s + taps(i, first_kb, KB)
        so[rows, :] = acc.astype(jnp.bfloat16)

    lax.fori_loop(0, 1, conv_a, 0)
    weights_on(2)
    lax.fori_loop(BURST, NRAW, start_raw, 0)
    lax.fori_loop(1, 3, conv_a, 0)
    weights_last(0)
    lax.fori_loop(3, 5, conv_a, 0)
    weights_last(1)
    lax.fori_loop(5, 7, conv_a, 0)
    weights_last(2)
    lax.fori_loop(7, NCH, conv_a, 0)
    for k in range(NSUB):
        weights_near(k)

    def conv_far(i):
        acc = taps(i, 0, D) + bias_s
        sf[pl.ds(pl.multiple_of(i * M, M), M), :] = acc.astype(jnp.bfloat16)

    def chunk(ref, i):
        return ref.at[pl.ds(pl.multiple_of(i * M, M), M), :]

    def to_sibling(i):
        return send(chunk(so, i), chunk(ss, i), sib_snd.at[i], sib_rcv.at[i], sibling)

    def to_partner(i):
        return send(chunk(so, i), chunk(sf, i), sp_snd.at[i], sp_rcv.at[i], partner)

    def shared_chunk(i, _):
        conv_b(i)
        to_partner(i).start()
        to_sibling(i).start()
        return 0

    lax.fori_loop(NRAW, NCH, shared_chunk, 0)

    def own_chunk(i, _):
        conv_b(i)
        to_sibling(i).start()
        return 0

    lax.fori_loop(0, NRAW, own_chunk, 0)

    far_tap = 9 + 2 * core
    near_tap = 11 - 2 * core

    def temporal(i):
        to_sibling(i).wait_recv()
        rows = pl.ds(pl.multiple_of(i * M, M), M)
        acc = xin[rows, :].astype(jnp.float32) + bias_t
        acc = acc + jnp.dot(so[rows, :], wts[10], preferred_element_type=jnp.float32)
        acc = acc + jnp.dot(ss[rows, :], wts[near_tap], preferred_element_type=jnp.float32)
        far = sf[rows, :]
        far = jnp.where(valid, far, jnp.zeros_like(far))
        acc = acc + jnp.dot(far, wts[far_tap], preferred_element_type=jnp.float32)
        out[rows, :] = acc.astype(jnp.bfloat16)

    pre.wait_recv()
    normalise_row(xf, 0)

    def raw_chunk(i, _):
        raw_copy(i).wait_recv()

        def one(j, _):
            normalise_row(xf, i * R + 1 + j)
            return 0

        lax.fori_loop(0, R, one, 0)
        conv_far(i)
        temporal(i)
        return 0

    lax.fori_loop(0, NRAW, raw_chunk, 0)

    def sent_chunk(i, _):
        to_partner(i).wait_recv()
        temporal(i)
        return 0

    lax.fori_loop(NRAW, NCH, sent_chunk, 0)

    for c in ones + twos + sent + [pre]:
        c.wait_send()

    def drain_raw(i, _):
        raw_copy(i).wait_send()
        return 0

    lax.fori_loop(0, NRAW, drain_raw, 0)

    def drain_partner(i, _):
        to_partner(i).wait_send()
        return 0

    lax.fori_loop(NRAW, NCH, drain_partner, 0)

    def drain_all(i, _):
        to_sibling(i).wait_send()
        return 0

    lax.fori_loop(0, NCH, drain_all, 0)


def shards(frames, norm_gain, norm_shift, spatial_weight, spatial_bias, temporal_weight, temporal_bias):
    vm = pl.BlockSpec(memory_space=pltpu.VMEM)
    hbm = pl.BlockSpec(memory_space=pl.ANY)
    dma = pltpu.SemaphoreType.DMA
    bf = jnp.bfloat16
    result = pl.pallas_call(
        kernel,
        out_shape=pltpu.VMEM((H * W, D), bf),
        in_specs=[hbm, vm, vm, hbm, vm, hbm, vm],
        out_specs=vm,
        scratch_shapes=[
            pltpu.VMEM((H * W, D), bf),
            pltpu.VMEM(((NRAW * R + 1) * W, D), bf),
            pltpu.VMEM((H * W, D), bf),
            pltpu.VMEM((H * W, D), bf),
            pltpu.VMEM((H * W, D), bf),
            pltpu.VMEM(((H + 2) * W, 3 * D), bf),
            pltpu.VMEM((12, D, D), bf),
            pltpu.VMEM((H * W, D), jnp.float32),
            pltpu.VMEM((2, D), jnp.float32),
            pltpu.VMEM((7, 2, D), jnp.float32),
            pltpu.VMEM((2, D), jnp.float32),
            pltpu.VMEM((7, 2, D), jnp.float32),
            dma((3,)), dma((NSUB, 10)), dma((NSUB, 10)), dma((14,)), dma((14,)),
            dma((NRAW + 1,)), dma((NRAW + 1,)), dma((NCH,)), dma((NCH,)),
            dma((NCH,)), dma((NCH,)),
        ],
        compiler_params=pltpu.CompilerParams(
            collective_id=0, has_side_effects=True, vmem_limit_bytes=56 * 2**20
        ),
    )(
        frames.reshape(H * W, D), norm_gain, norm_shift,
        spatial_weight.reshape(9, HALF, D), spatial_bias, temporal_weight, temporal_bias,
    )
    return result.reshape(1, 1, H, W, D)


def solution(mesh):
    in_specs = (
        P("dp", "tm", None, None, None),
        P(),
        P(),
        P(None, None, "dp", None),
        P(),
        P(None, "dp", None),
        P(),
    )
    out_specs = P("dp", "tm", None, None, None)
    return jax.shard_map(shards, mesh=mesh, in_specs=in_specs, out_specs=out_specs, check_vma=False)
```

```python
import functools

import jax
import jax.numpy as jnp
from jax import lax
from jax.experimental import pallas as pl
from jax.experimental.pallas import tpu as pltpu
from jax.sharding import PartitionSpec as P

MESH = pl.DeviceIdType.MESH
GROUPS = 32
D = 640
H = 36
W = 64
HALF = D // 2
QUART = HALF // 4
R = 4
NCH = H // R
NRAW = 4
SERVE = 5
KA = 256
KB = D - KA
M = R * W
MEMBERS = 64 * H * W * (D // GROUPS)


def device(x, y, z, core):
    x, y, z = lax.rem(x + 4, 4), lax.rem(y + 4, 4), lax.rem(z + 4, 4)
    return lax.rem(x, 2), ((z * 4 + y) * 2 + x // 2) * 2 + core


def kernel(
    frames, gain, shift, sw, sb, tw, tb, out,
    xin, xf, sf, so, ss, hid, wts, partial,
    st, rs1, tot1, rs2,
    lsem, wsnd, wrcv, st_snd, st_rcv, raw_snd, raw_rcv, sp_snd, sp_rcv, sib_snd, sib_rcv,
):
    dp = lax.axis_index("dp")
    tm = lax.axis_index("tm")
    core = lax.rem(tm, 2)
    xh = lax.rem(tm // 2, 2)
    y = lax.rem(tm // 4, 4)
    z = tm // 16
    x = xh * 2 + dp
    other = 1 - dp

    sibling = (dp, tm + 1 - 2 * core)
    partner = (dp, lax.rem(tm + 2 * core - 1 + 64, 64))
    valid = jnp.logical_and(tm > 0, tm < 63)
    x_to = device(x + 2 * core - 1, y, z, core)
    x_from = device(x + 1 - 2 * core, y, z, core)
    up = device(x, y + 1 - core, z + core, core)
    down = device(x, y - 1 + core, z - core, core)
    pos = y * (1 - core) + z * core
    g1 = y * 2 + core
    g2 = z * 2 + xh

    def first_group(k):
        g = lax.rem(g1 + k, 8)
        return device(x, g // 2, z, lax.rem(g, 2))

    def second_group(k):
        g = lax.rem(g2 + k, 8)
        return device(lax.rem(g, 2) * 2 + dp, y, g // 2, core)

    load_x = pltpu.make_async_copy(frames, xin, lsem.at[0])
    mine = pl.ds(pl.multiple_of(dp * HALF, 16), HALF)
    load_s = pltpu.make_async_copy(sw, wts.at[pl.ds(0, 9), mine, :], lsem.at[1])
    load_t = pltpu.make_async_copy(tw, wts.at[pl.ds(9, 3), mine, :], lsem.at[2])
    load_s.start()
    load_t.start()
    load_x.start()

    barrier = pltpu.get_barrier_semaphore()
    greet = [sibling, partner, x_to, x_from, up, down]
    greet += [first_group(k) for k in range(1, 8)] + [second_group(k) for k in range(1, 8)]
    for who in greet:
        pl.semaphore_signal(barrier, inc=1, device_id=who, device_id_type=MESH)
    pl.semaphore_wait(barrier, len(greet))

    def send(src, dst, ssem, rsem, who):
        return pltpu.make_async_remote_copy(
            src_ref=src, dst_ref=dst, send_sem=ssem, recv_sem=rsem, device_id=who, device_id_type=MESH
        )

    def part(half, owner_core, q, first=0, count=6):
        rows = pl.ds(pl.multiple_of(half * HALF + lax.rem(q + 4, 4) * QUART, 16), QUART)
        return wts.at[pl.ds(owner_core * 6 + first, count), rows, :]

    def wcopy(piece, i, who):
        return send(piece, piece, wsnd.at[i], wrcv.at[i], who)

    load_s.wait()
    load_t.wait()
    x_out = wcopy(part(dp, core, pos), 0, x_to)
    x_out.start()

    pre = send(frames.at[pl.ds(0, W), :], xf.at[pl.ds(0, W), :], raw_snd.at[NRAW], raw_rcv.at[NRAW], partner)

    def raw_copy(i):
        rows = pl.ds(pl.multiple_of(i * M + W, W), M)
        return send(frames.at[rows, :], xf.at[rows, :], raw_snd.at[i], raw_rcv.at[i], partner)

    def start_raw(i, _):
        raw_copy(i).start()
        return 0

    load_x.wait()

    def add_rows(i, carry):
        s, q = carry
        v = xin[pl.ds(pl.multiple_of(i * W, W), W), :].astype(jnp.float32).reshape(W // 8, 8, D)
        return s + jnp.sum(v, axis=0), q + jnp.sum(v * v, axis=0)

    zero = jnp.zeros((8, D), jnp.float32)
    s, q = lax.fori_loop(0, H, add_rows, (zero, zero))
    st[0:1, :] = jnp.sum(s, axis=0, keepdims=True)
    st[1:2, :] = jnp.sum(q, axis=0, keepdims=True)
    ones = []
    for k in range(1, 8):
        ones.append(send(st, rs1.at[k - 1], st_snd.at[k - 1], st_rcv.at[k - 1], first_group(k)))
        ones[-1].start()
    hid[0:W, :] = jnp.zeros((W, 3 * D), jnp.bfloat16)
    hid[(H + 1) * W:(H + 2) * W, :] = jnp.zeros((W, 3 * D), jnp.bfloat16)
    x_out.wait_send()
    for c in ones:
        c.wait_recv()
    tot1[...] = st[...] + jnp.sum(rs1[...], axis=0)
    twos = []
    for k in range(1, 8):
        twos.append(send(tot1, rs2.at[k - 1], st_snd.at[k + 6], st_rcv.at[k + 6], second_group(k)))
        twos[-1].start()

    wcopy(part(other, core, pos), 0, x_to).wait_recv()
    theirs = 1 - core
    ring = [
        wcopy(part(other, core, pos), 1, up),
        wcopy(part(other, core, pos), 2, down),
        wcopy(part(other, core, pos), 5, sibling),
    ]
    for c in ring:
        c.start()
    pre.start()
    lax.fori_loop(0, 2, start_raw, 0)

    for c in twos:
        c.wait_recv()
    total = tot1[...] + jnp.sum(rs2[...], axis=0)

    ch = lax.broadcasted_iota(jnp.int32, (D, 128), 0)
    gr = lax.broadcasted_iota(jnp.int32, (D, 128), 1) * (D // GROUPS)
    member = jnp.logical_and(ch >= gr, ch < gr + D // GROUPS).astype(jnp.float32)
    ch_t = lax.broadcasted_iota(jnp.int32, (128, D), 1)
    gr_t = lax.broadcasted_iota(jnp.int32, (128, D), 0) * (D // GROUPS)
    spread = jnp.logical_and(ch_t >= gr_t, ch_t < gr_t + D // GROUPS).astype(jnp.float32)
    eight = jnp.concatenate([total, jnp.zeros((6, D), jnp.float32)], axis=0)
    per_group = jnp.dot(
        eight, member, precision=lax.Precision.HIGHEST, preferred_element_type=jnp.float32
    ) * (1.0 / MEMBERS)
    average = per_group[0:1, :]
    inv = lax.rsqrt(per_group[1:2, :] - average * average + 1e-5)
    pair = jnp.concatenate([average, inv, jnp.zeros((6, 128), jnp.float32)], axis=0)
    pair = jnp.dot(pair, spread, precision=lax.Precision.HIGHEST, preferred_element_type=jnp.float32)
    scale = pair[1:2, :] * gain[...].reshape(1, D)
    half_scale = scale * 0.5
    half_shift = (shift[...].reshape(1, D) - pair[0:1, :] * scale) * 0.5
    bias_s = sb[...].reshape(1, D)
    bias_t = tb[...].reshape(1, D)

    col = lax.broadcasted_iota(jnp.int32, (W, 128), 0)
    not_first = col > 0
    not_last = col < W - 1

    def normalise_row(src, row):
        base = pl.multiple_of(row * W, W)
        to = pl.ds(pl.multiple_of((row + 1) * W, W), W)
        for b in range(D // 128):
            lanes = slice(b * 128, (b + 1) * 128)
            v = src[pl.ds(base, W), lanes].astype(jnp.float32)
            u = v * half_scale[:, lanes] + half_shift[:, lanes]
            h = u + u * jnp.tanh(u)
            before = jnp.where(not_first, pltpu.roll(h, 1, 0), 0.0)
            after = jnp.where(not_last, pltpu.roll(h, W - 1, 0), 0.0)
            hid[to, lanes] = before.astype(jnp.bfloat16)
            hid[to, D + b * 128:D + (b + 1) * 128] = h.astype(jnp.bfloat16)
            hid[to, 2 * D + b * 128:2 * D + (b + 1) * 128] = after.astype(jnp.bfloat16)

    def own_row(i, _):
        normalise_row(xin, i)
        return 0

    lax.fori_loop(0, H, own_row, 0)

    first_ka = pl.multiple_of(dp * KB, 128)
    first_kb = pl.multiple_of((1 - dp) * KA, 128)

    def taps(i, start, count):
        left = []
        for a in range(3):
            rows = pl.ds(pl.multiple_of(i * M + a * W, W), M)
            for b in range(3):
                left.append(hid[rows, pl.ds(pl.multiple_of(b * D + start, 128), count)])
        left = jnp.concatenate(left, axis=1)
        right = wts[0:9, pl.ds(start, count), :].reshape(9 * count, D)
        return jnp.dot(left, right, preferred_element_type=jnp.float32)

    def conv_a(i, _):
        partial[pl.ds(pl.multiple_of(i * M, M), M), :] = taps(i, first_ka, KA)
        return 0

    def conv_b(i):
        rows = pl.ds(pl.multiple_of(i * M, M), M)
        acc = partial[rows, :] + bias_s + taps(i, first_kb, KB)
        so[rows, :] = acc.astype(jnp.bfloat16)

    lax.fori_loop(0, SERVE, conv_a, 0)

    wcopy(part(other, core, pos - 1), 1, up).wait_recv()
    more = [wcopy(part(other, core, pos - 1, 0, 3), 3, up), wcopy(part(other, core, pos - 1), 6, sibling)]
    for c in more:
        c.start()
    wcopy(part(other, core, pos + 1), 2, down).wait_recv()
    more2 = [wcopy(part(other, core, pos + 1, 3, 3), 4, down), wcopy(part(other, core, pos + 1), 7, sibling)]
    for c in more2:
        c.start()
    lax.fori_loop(2, NRAW, start_raw, 0)

    lax.fori_loop(SERVE, NCH, conv_a, 0)

    wcopy(part(other, core, pos + 2, 0, 3), 3, up).wait_recv()
    last = [wcopy(part(other, core, pos + 2, 0, 3), 8, sibling)]
    last[0].start()
    wcopy(part(other, core, pos + 2, 3, 3), 4, down).wait_recv()
    last.append(wcopy(part(other, core, pos + 2, 3, 3), 9, sibling))
    last[1].start()
    their_pos = y * (1 - theirs) + z * theirs
    for piece, i in (
        (part(other, theirs, their_pos), 5),
        (part(other, theirs, their_pos - 1), 6),
        (part(other, theirs, their_pos + 1), 7),
        (part(other, theirs, their_pos + 2, 0, 3), 8),
        (part(other, theirs, their_pos + 2, 3, 3), 9),
    ):
        wcopy(piece, i, sibling).wait_recv()

    def conv_far(i):
        acc = taps(i, 0, D) + bias_s
        sf[pl.ds(pl.multiple_of(i * M, M), M), :] = acc.astype(jnp.bfloat16)

    def chunk(ref, i):
        return ref.at[pl.ds(pl.multiple_of(i * M, M), M), :]

    def to_sibling(i):
        return send(chunk(so, i), chunk(ss, i), sib_snd.at[i], sib_rcv.at[i], sibling)

    def to_partner(i):
        return send(chunk(so, i), chunk(sf, i), sp_snd.at[i], sp_rcv.at[i], partner)

    def shared_chunk(i, _):
        conv_b(i)
        to_partner(i).start()
        to_sibling(i).start()
        return 0

    lax.fori_loop(NRAW, NCH, shared_chunk, 0)

    def own_chunk(i, _):
        conv_b(i)
        to_sibling(i).start()
        return 0

    lax.fori_loop(0, NRAW, own_chunk, 0)

    far_tap = 9 + 2 * core
    near_tap = 11 - 2 * core

    def temporal(i):
        to_sibling(i).wait_recv()
        rows = pl.ds(pl.multiple_of(i * M, M), M)
        acc = xin[rows, :].astype(jnp.float32) + bias_t
        acc = acc + jnp.dot(so[rows, :], wts[10], preferred_element_type=jnp.float32)
        acc = acc + jnp.dot(ss[rows, :], wts[near_tap], preferred_element_type=jnp.float32)
        far = sf[rows, :]
        far = jnp.where(valid, far, jnp.zeros_like(far))
        acc = acc + jnp.dot(far, wts[far_tap], preferred_element_type=jnp.float32)
        out[rows, :] = acc.astype(jnp.bfloat16)

    pre.wait_recv()
    normalise_row(xf, 0)

    def raw_chunk(i, _):
        raw_copy(i).wait_recv()

        def one(j, _):
            normalise_row(xf, i * R + 1 + j)
            return 0

        lax.fori_loop(0, R, one, 0)
        conv_far(i)
        temporal(i)
        return 0

    lax.fori_loop(0, NRAW, raw_chunk, 0)

    def sent_chunk(i, _):
        to_partner(i).wait_recv()
        temporal(i)
        return 0

    lax.fori_loop(NRAW, NCH, sent_chunk, 0)

    for c in ones + twos + ring + more + more2 + last + [pre]:
        c.wait_send()

    def drain_raw(i, _):
        raw_copy(i).wait_send()
        return 0

    lax.fori_loop(0, NRAW, drain_raw, 0)

    def drain_partner(i, _):
        to_partner(i).wait_send()
        return 0

    lax.fori_loop(NRAW, NCH, drain_partner, 0)

    def drain_all(i, _):
        to_sibling(i).wait_send()
        return 0

    lax.fori_loop(0, NCH, drain_all, 0)


def shards(frames, norm_gain, norm_shift, spatial_weight, spatial_bias, temporal_weight, temporal_bias):
    vm = pl.BlockSpec(memory_space=pltpu.VMEM)
    hbm = pl.BlockSpec(memory_space=pl.ANY)
    dma = pltpu.SemaphoreType.DMA
    bf = jnp.bfloat16
    result = pl.pallas_call(
        kernel,
        out_shape=pltpu.VMEM((H * W, D), bf),
        in_specs=[hbm, vm, vm, hbm, vm, hbm, vm],
        out_specs=vm,
        scratch_shapes=[
            pltpu.VMEM((H * W, D), bf),
            pltpu.VMEM(((NRAW * R + 1) * W, D), bf),
            pltpu.VMEM((H * W, D), bf),
            pltpu.VMEM((H * W, D), bf),
            pltpu.VMEM((H * W, D), bf),
            pltpu.VMEM(((H + 2) * W, 3 * D), bf),
            pltpu.VMEM((12, D, D), bf),
            pltpu.VMEM((H * W, D), jnp.float32),
            pltpu.VMEM((2, D), jnp.float32),
            pltpu.VMEM((7, 2, D), jnp.float32),
            pltpu.VMEM((2, D), jnp.float32),
            pltpu.VMEM((7, 2, D), jnp.float32),
            dma((3,)), dma((10,)), dma((10,)), dma((14,)), dma((14,)),
            dma((NRAW + 1,)), dma((NRAW + 1,)), dma((NCH,)), dma((NCH,)),
            dma((NCH,)), dma((NCH,)),
        ],
        compiler_params=pltpu.CompilerParams(
            collective_id=0, has_side_effects=True, vmem_limit_bytes=56 * 2**20
        ),
    )(
        frames.reshape(H * W, D), norm_gain, norm_shift,
        spatial_weight.reshape(9, HALF, D), spatial_bias, temporal_weight, temporal_bias,
    )
    return result.reshape(1, 1, H, W, D)


def solution(mesh):
    in_specs = (
        P("dp", "tm", None, None, None),
        P(),
        P(),
        P(None, None, "dp", None),
        P(),
        P(None, "dp", None),
        P(),
    )
    out_specs = P("dp", "tm", None, None, None)
    return jax.shard_map(shards, mesh=mesh, in_specs=in_specs, out_specs=out_specs, check_vma=False)
```

```python
import functools

import jax
import jax.numpy as jnp
from jax import lax
from jax.experimental import pallas as pl
from jax.experimental.pallas import tpu as pltpu
from jax.sharding import PartitionSpec as P

MESH = pl.DeviceIdType.MESH
GROUPS = 32
D = 640
H = 36
W = 64
HALF = D // 2
QUART = HALF // 4
R = 4
NCH = H // R
NRAW = 4
SERVE = 5
KA = 256
KB = D - KA
M = R * W
MEMBERS = 64 * H * W * (D // GROUPS)


def device(x, y, z, core):
    x, y, z = lax.rem(x + 4, 4), lax.rem(y + 4, 4), lax.rem(z + 4, 4)
    return lax.rem(x, 2), ((z * 4 + y) * 2 + x // 2) * 2 + core


def kernel(
    frames, gain, shift, sw, sb, tw, tb, out,
    xin, xf, sf, so, ss, hid, wts, partial,
    st, rs1, tot1, rs2,
    lsem, wsnd, wrcv, st_snd, st_rcv, raw_snd, raw_rcv, sp_snd, sp_rcv, sib_snd, sib_rcv,
):
    dp = lax.axis_index("dp")
    tm = lax.axis_index("tm")
    core = lax.rem(tm, 2)
    xh = lax.rem(tm // 2, 2)
    y = lax.rem(tm // 4, 4)
    z = tm // 16
    x = xh * 2 + dp
    other = 1 - dp

    sibling = (dp, tm + 1 - 2 * core)
    partner = (dp, lax.rem(tm + 2 * core - 1 + 64, 64))
    valid = jnp.logical_and(tm > 0, tm < 63)
    x_to = device(x + 2 * core - 1, y, z, core)
    x_from = device(x + 1 - 2 * core, y, z, core)
    up = device(x, y + 1 - core, z + core, core)
    down = device(x, y - 1 + core, z - core, core)
    pos = y * (1 - core) + z * core
    g1 = y * 2 + core
    g2 = z * 2 + xh

    def first_group(k):
        g = lax.rem(g1 + k, 8)
        return device(x, g // 2, z, lax.rem(g, 2))

    def second_group(k):
        g = lax.rem(g2 + k, 8)
        return device(lax.rem(g, 2) * 2 + dp, y, g // 2, core)

    load_x = pltpu.make_async_copy(frames, xin, lsem.at[0])
    mine = pl.ds(pl.multiple_of(dp * HALF, 16), HALF)
    load_s = pltpu.make_async_copy(sw, wts.at[pl.ds(0, 9), mine, :], lsem.at[1])
    load_t = pltpu.make_async_copy(tw, wts.at[pl.ds(9, 3), mine, :], lsem.at[2])
    load_s.start()
    load_t.start()

    barrier = pltpu.get_barrier_semaphore()
    greet = [sibling, partner, x_to, x_from, up, down]
    greet += [first_group(k) for k in range(1, 8)] + [second_group(k) for k in range(1, 8)]
    for who in greet:
        pl.semaphore_signal(barrier, inc=1, device_id=who, device_id_type=MESH)
    pl.semaphore_wait(barrier, len(greet))

    def send(src, dst, ssem, rsem, who):
        return pltpu.make_async_remote_copy(
            src_ref=src, dst_ref=dst, send_sem=ssem, recv_sem=rsem, device_id=who, device_id_type=MESH
        )

    def part(half, owner_core, q, first=0, count=6):
        rows = pl.ds(pl.multiple_of(half * HALF + lax.rem(q + 4, 4) * QUART, 16), QUART)
        return wts.at[pl.ds(owner_core * 6 + first, count), rows, :]

    def wcopy(piece, i, who):
        return send(piece, piece, wsnd.at[i], wrcv.at[i], who)

    load_s.wait()
    load_t.wait()
    x_out = wcopy(part(dp, core, pos), 0, x_to)
    x_out.start()
    load_x.start()

    pre = send(frames.at[pl.ds(0, W), :], xf.at[pl.ds(0, W), :], raw_snd.at[NRAW], raw_rcv.at[NRAW], partner)

    def raw_copy(i):
        rows = pl.ds(pl.multiple_of(i * M + W, W), M)
        return send(frames.at[rows, :], xf.at[rows, :], raw_snd.at[i], raw_rcv.at[i], partner)

    def start_raw(i, _):
        raw_copy(i).start()
        return 0

    load_x.wait()

    def add_rows(i, carry):
        s, q = carry
        v = xin[pl.ds(pl.multiple_of(i * W, W), W), :].astype(jnp.float32).reshape(W // 8, 8, D)
        return s + jnp.sum(v, axis=0), q + jnp.sum(v * v, axis=0)

    zero = jnp.zeros((8, D), jnp.float32)
    s, q = lax.fori_loop(0, H, add_rows, (zero, zero))
    st[0:1, :] = jnp.sum(s, axis=0, keepdims=True)
    st[1:2, :] = jnp.sum(q, axis=0, keepdims=True)
    ones = []
    for k in range(1, 8):
        ones.append(send(st, rs1.at[k - 1], st_snd.at[k - 1], st_rcv.at[k - 1], first_group(k)))
        ones[-1].start()
    hid[0:W, :] = jnp.zeros((W, 3 * D), jnp.bfloat16)
    hid[(H + 1) * W:(H + 2) * W, :] = jnp.zeros((W, 3 * D), jnp.bfloat16)
    x_out.wait_send()
    for c in ones:
        c.wait_recv()
    tot1[...] = st[...] + jnp.sum(rs1[...], axis=0)
    twos = []
    for k in range(1, 8):
        twos.append(send(tot1, rs2.at[k - 1], st_snd.at[k + 6], st_rcv.at[k + 6], second_group(k)))
        twos[-1].start()

    wcopy(part(other, core, pos), 0, x_to).wait_recv()
    theirs = 1 - core
    ring = [
        wcopy(part(other, core, pos), 1, up),
        wcopy(part(other, core, pos), 2, down),
        wcopy(part(other, core, pos), 5, sibling),
    ]
    for c in ring:
        c.start()
    pre.start()
    lax.fori_loop(0, 2, start_raw, 0)

    for c in twos:
        c.wait_recv()
    total = tot1[...] + jnp.sum(rs2[...], axis=0)

    ch = lax.broadcasted_iota(jnp.int32, (D, 128), 0)
    gr = lax.broadcasted_iota(jnp.int32, (D, 128), 1) * (D // GROUPS)
    member = jnp.logical_and(ch >= gr, ch < gr + D // GROUPS).astype(jnp.float32)
    ch_t = lax.broadcasted_iota(jnp.int32, (128, D), 1)
    gr_t = lax.broadcasted_iota(jnp.int32, (128, D), 0) * (D // GROUPS)
    spread = jnp.logical_and(ch_t >= gr_t, ch_t < gr_t + D // GROUPS).astype(jnp.float32)
    eight = jnp.concatenate([total, jnp.zeros((6, D), jnp.float32)], axis=0)
    per_group = jnp.dot(
        eight, member, precision=lax.Precision.HIGHEST, preferred_element_type=jnp.float32
    ) * (1.0 / MEMBERS)
    average = per_group[0:1, :]
    inv = lax.rsqrt(per_group[1:2, :] - average * average + 1e-5)
    pair = jnp.concatenate([average, inv, jnp.zeros((6, 128), jnp.float32)], axis=0)
    pair = jnp.dot(pair, spread, precision=lax.Precision.HIGHEST, preferred_element_type=jnp.float32)
    scale = pair[1:2, :] * gain[...].reshape(1, D)
    half_scale = scale * 0.5
    half_shift = (shift[...].reshape(1, D) - pair[0:1, :] * scale) * 0.5
    bias_s = sb[...].reshape(1, D)
    bias_t = tb[...].reshape(1, D)

    col = lax.broadcasted_iota(jnp.int32, (W, 128), 0)
    not_first = col > 0
    not_last = col < W - 1

    def normalise_row(src, row):
        base = pl.multiple_of(row * W, W)
        to = pl.ds(pl.multiple_of((row + 1) * W, W), W)
        for b in range(D // 128):
            lanes = slice(b * 128, (b + 1) * 128)
            v = src[pl.ds(base, W), lanes].astype(jnp.float32)
            u = v * half_scale[:, lanes] + half_shift[:, lanes]
            h = u + u * jnp.tanh(u)
            before = jnp.where(not_first, pltpu.roll(h, 1, 0), 0.0)
            after = jnp.where(not_last, pltpu.roll(h, W - 1, 0), 0.0)
            hid[to, lanes] = before.astype(jnp.bfloat16)
            hid[to, D + b * 128:D + (b + 1) * 128] = h.astype(jnp.bfloat16)
            hid[to, 2 * D + b * 128:2 * D + (b + 1) * 128] = after.astype(jnp.bfloat16)

    def own_row(i, _):
        normalise_row(xin, i)
        return 0

    lax.fori_loop(0, H, own_row, 0)

    first_ka = pl.multiple_of(dp * KB, 128)
    first_kb = pl.multiple_of((1 - dp) * KA, 128)

    def taps(i, start, count):
        left = []
        for a in range(3):
            rows = pl.ds(pl.multiple_of(i * M + a * W, W), M)
            for b in range(3):
                left.append(hid[rows, pl.ds(pl.multiple_of(b * D + start, 128), count)])
        left = jnp.concatenate(left, axis=1)
        right = wts[0:9, pl.ds(start, count), :].reshape(9 * count, D)
        return jnp.dot(left, right, preferred_element_type=jnp.float32)

    def conv_a(i, _):
        partial[pl.ds(pl.multiple_of(i * M, M), M), :] = taps(i, first_ka, KA)
        return 0

    def conv_b(i):
        rows = pl.ds(pl.multiple_of(i * M, M), M)
        acc = partial[rows, :] + bias_s + taps(i, first_kb, KB)
        so[rows, :] = acc.astype(jnp.bfloat16)

    lax.fori_loop(0, SERVE, conv_a, 0)

    wcopy(part(other, core, pos - 1), 1, up).wait_recv()
    more = [wcopy(part(other, core, pos - 1, 0, 3), 3, up), wcopy(part(other, core, pos - 1), 6, sibling)]
    for c in more:
        c.start()
    wcopy(part(other, core, pos + 1), 2, down).wait_recv()
    more2 = [wcopy(part(other, core, pos + 1, 3, 3), 4, down), wcopy(part(other, core, pos + 1), 7, sibling)]
    for c in more2:
        c.start()
    lax.fori_loop(2, NRAW, start_raw, 0)

    lax.fori_loop(SERVE, NCH, conv_a, 0)

    wcopy(part(other, core, pos + 2, 0, 3), 3, up).wait_recv()
    last = [wcopy(part(other, core, pos + 2, 0, 3), 8, sibling)]
    last[0].start()
    wcopy(part(other, core, pos + 2, 3, 3), 4, down).wait_recv()
    last.append(wcopy(part(other, core, pos + 2, 3, 3), 9, sibling))
    last[1].start()
    their_pos = y * (1 - theirs) + z * theirs
    for piece, i in (
        (part(other, theirs, their_pos), 5),
        (part(other, theirs, their_pos - 1), 6),
        (part(other, theirs, their_pos + 1), 7),
        (part(other, theirs, their_pos + 2, 0, 3), 8),
        (part(other, theirs, their_pos + 2, 3, 3), 9),
    ):
        wcopy(piece, i, sibling).wait_recv()

    def conv_far(i):
        acc = taps(i, 0, D) + bias_s
        sf[pl.ds(pl.multiple_of(i * M, M), M), :] = acc.astype(jnp.bfloat16)

    def chunk(ref, i):
        return ref.at[pl.ds(pl.multiple_of(i * M, M), M), :]

    def to_sibling(i):
        return send(chunk(so, i), chunk(ss, i), sib_snd.at[i], sib_rcv.at[i], sibling)

    def to_partner(i):
        return send(chunk(so, i), chunk(sf, i), sp_snd.at[i], sp_rcv.at[i], partner)

    def shared_chunk(i, _):
        conv_b(i)
        to_partner(i).start()
        to_sibling(i).start()
        return 0

    lax.fori_loop(NRAW, NCH, shared_chunk, 0)

    def own_chunk(i, _):
        conv_b(i)
        to_sibling(i).start()
        return 0

    lax.fori_loop(0, NRAW, own_chunk, 0)

    far_tap = 9 + 2 * core
    near_tap = 11 - 2 * core

    def temporal(i):
        to_sibling(i).wait_recv()
        rows = pl.ds(pl.multiple_of(i * M, M), M)
        acc = xin[rows, :].astype(jnp.float32) + bias_t
        acc = acc + jnp.dot(so[rows, :], wts[10], preferred_element_type=jnp.float32)
        acc = acc + jnp.dot(ss[rows, :], wts[near_tap], preferred_element_type=jnp.float32)
        far = sf[rows, :]
        far = jnp.where(valid, far, jnp.zeros_like(far))
        acc = acc + jnp.dot(far, wts[far_tap], preferred_element_type=jnp.float32)
        out[rows, :] = acc.astype(jnp.bfloat16)

    pre.wait_recv()
    normalise_row(xf, 0)

    def raw_chunk(i, _):
        raw_copy(i).wait_recv()

        def one(j, _):
            normalise_row(xf, i * R + 1 + j)
            return 0

        lax.fori_loop(0, R, one, 0)
        conv_far(i)
        temporal(i)
        return 0

    lax.fori_loop(0, NRAW, raw_chunk, 0)

    def sent_chunk(i, _):
        to_partner(i).wait_recv()
        temporal(i)
        return 0

    lax.fori_loop(NRAW, NCH, sent_chunk, 0)

    for c in ones + twos + ring + more + more2 + last + [pre]:
        c.wait_send()

    def drain_raw(i, _):
        raw_copy(i).wait_send()
        return 0

    lax.fori_loop(0, NRAW, drain_raw, 0)

    def drain_partner(i, _):
        to_partner(i).wait_send()
        return 0

    lax.fori_loop(NRAW, NCH, drain_partner, 0)

    def drain_all(i, _):
        to_sibling(i).wait_send()
        return 0

    lax.fori_loop(0, NCH, drain_all, 0)


def shards(frames, norm_gain, norm_shift, spatial_weight, spatial_bias, temporal_weight, temporal_bias):
    vm = pl.BlockSpec(memory_space=pltpu.VMEM)
    hbm = pl.BlockSpec(memory_space=pl.ANY)
    dma = pltpu.SemaphoreType.DMA
    bf = jnp.bfloat16
    result = pl.pallas_call(
        kernel,
        out_shape=pltpu.VMEM((H * W, D), bf),
        in_specs=[hbm, vm, vm, hbm, vm, hbm, vm],
        out_specs=vm,
        scratch_shapes=[
            pltpu.VMEM((H * W, D), bf),
            pltpu.VMEM(((NRAW * R + 1) * W, D), bf),
            pltpu.VMEM((H * W, D), bf),
            pltpu.VMEM((H * W, D), bf),
            pltpu.VMEM((H * W, D), bf),
            pltpu.VMEM(((H + 2) * W, 3 * D), bf),
            pltpu.VMEM((12, D, D), bf),
            pltpu.VMEM((H * W, D), jnp.float32),
            pltpu.VMEM((2, D), jnp.float32),
            pltpu.VMEM((7, 2, D), jnp.float32),
            pltpu.VMEM((2, D), jnp.float32),
            pltpu.VMEM((7, 2, D), jnp.float32),
            dma((3,)), dma((10,)), dma((10,)), dma((14,)), dma((14,)),
            dma((NRAW + 1,)), dma((NRAW + 1,)), dma((NCH,)), dma((NCH,)),
            dma((NCH,)), dma((NCH,)),
        ],
        compiler_params=pltpu.CompilerParams(
            collective_id=0, has_side_effects=True, vmem_limit_bytes=56 * 2**20
        ),
    )(
        frames.reshape(H * W, D), norm_gain, norm_shift,
        spatial_weight.reshape(9, HALF, D), spatial_bias, temporal_weight, temporal_bias,
    )
    return result.reshape(1, 1, H, W, D)


def solution(mesh):
    in_specs = (
        P("dp", "tm", None, None, None),
        P(),
        P(),
        P(None, None, "dp", None),
        P(),
        P(None, "dp", None),
        P(),
    )
    out_specs = P("dp", "tm", None, None, None)
    return jax.shard_map(shards, mesh=mesh, in_specs=in_specs, out_specs=out_specs, check_vma=False)
```
